32 devices in a mesh: row: 16 (over z, y, core), col: 2 (over x).
Axes of the slice: x: 2, y: 2, z: 4, core: 2. Of those that a mesh axis runs over, the one named last changes fastest.
Arguments:
- image_tokens: bfloat16 [8192, 2, 1536], P('row', 'col'), may hold values from -6 to 6
- text_tokens: bfloat16 [1232, 2, 1536], P('row', 'col'), may hold values from -6 to 6
- conditioning: float32 [16, 1536], P('row', 'col'), may hold values from -6 to 6
- ada_weight: float32 [1536, 2, 9216], P('row', 'col'), may hold values from -0.15625 to 0.15625
- qkv_weight: float32 [1536, 2, 4608], P('row', 'col'), may hold values from -0.15625 to 0.15625
- proj_weight: float32 [1536, 2, 1536], P('row', 'col'), may hold values from -0.625 to 0.625
- fc1_weight: float32 [1536, 2, 6144], P('row', None, 'col'), may hold values from -0.15625 to 0.15625
- fc2_weight: float32 [6144, 2, 1536], P('row', 'col'), may hold values from -0.078125 to 0.078125
- image_cotangent: bfloat16 [8192, 2, 1536], P('row', 'col'), may hold values from -6 to 6
- text_cotangent: bfloat16 [1232, 2, 1536], P('row', 'col'), may hold values from -6 to 6
Outputs:
- image_out: bfloat16 [8192, 2, 1536], P('row', 'col')
- text_out: bfloat16 [1232, 2, 1536], P('row', 'col')
- grad_image: float32 [8192, 2, 1536], P('row', 'col')
- grad_text: float32 [1232, 2, 1536], P('row', 'col')
- grad_cond: float32 [16, 1536], P('row', 'col')
- grad_ada: float32 [1536, 2, 9216], P('row', 'col')
- grad_qkv: float32 [1536, 2, 4608], P('row', 'col')
- grad_proj: float32 [1536, 2, 1536], P('row', 'col')
- grad_fc1: float32 [1536, 2, 6144], P('row', None, 'col')
- grad_fc2: float32 [6144, 2, 1536], P('row', 'col')
The draws below stay inside these ranges and needn't reach their ends.
All inputs are finite; a program needn't handle non-finite values.
Results may differ from the reference program's by a relative error of at most 0.015.
The reference program's roundings to bfloat16 on the way count: a program that leaves them out, or rounds other values in their place, can miss the bound.
Values may be sent and summed in bfloat16 or wider, within the bound.
No kernel may reach another device: no remote copies, remote signals or barrier semaphores. Data moves between devices by JAX's collectives and lax.ppermute only.
A program may use at most 448 MiB of HBM per device.

```python
import jax
import jax.numpy as jnp
from jax import lax

MODEL_WIDTH = 1536
HEADS = 24
HEAD_DIM = 64
FEEDFORWARD_UNITS = 6144
IMG = 1024
TXT = 154
SEQS = 16
IMAGE_ROWS = 16384
TEXT_ROWS = 2464
N_COL = 2


def levels(stream_key, shape, shards, low, top_value):
    def one(position, shards_of):
        heights = jax.random.uniform(jax.random.fold_in(jax.random.fold_in(stream_key, 6), position), (shards_of,), jnp.float32, low / len(shards), top_value / len(shards))
        return jnp.repeat(jnp.exp(heights), shape[position] // shards_of).reshape((-1,) + (1,) * (len(shape) - position - 1))

    level = one(*shards[0])
    for cut in shards[1:]:
        level = level * one(*cut)
    return level


def centred(own_key, dims, spread, reach, cuts=(), held_as=jnp.bfloat16):
    loudness = levels(own_key, dims, cuts, -0.22, 0.18) if cuts else 1.0
    values = jax.random.normal(own_key, dims, jnp.float32) * spread * loudness
    return jnp.minimum(jnp.maximum(values, -reach), reach).astype(held_as)


def setup_inputs(seed: int = 0) -> dict:
    streams_of = jax.random.split(jax.random.key(seed), 11)
    image_tokens = centred(streams_of[0], (IMAGE_ROWS // 2, N_COL, 2 * MODEL_WIDTH // N_COL), 1.0, 6.0, ((0, 16), (1, 2)))
    text_tokens = centred(streams_of[1], (TEXT_ROWS // 2, N_COL, 2 * MODEL_WIDTH // N_COL), 1.0, 6.0, ((0, 16), (1, 2)))
    conditioning = centred(streams_of[2], (SEQS, MODEL_WIDTH), 1.0, 6.0, ((0, 16), (1, 2)), jnp.float32)
    ada_weight = centred(streams_of[3], (MODEL_WIDTH, N_COL, 12 * MODEL_WIDTH // N_COL), MODEL_WIDTH ** -0.5, 0.15625, ((0, 16), (1, 2)), jnp.float32)
    qkv_weight = centred(streams_of[4], (MODEL_WIDTH, N_COL, 6 * MODEL_WIDTH // N_COL), MODEL_WIDTH ** -0.5, 0.15625, ((0, 16), (1, 2)), jnp.float32)
    proj_weight = centred(streams_of[5], (MODEL_WIDTH, N_COL, 2 * MODEL_WIDTH // N_COL), (MODEL_WIDTH // 16) ** -0.5, 0.625, ((0, 16), (1, 2)), jnp.float32)
    fc1_weight = centred(streams_of[6], (MODEL_WIDTH, 2, FEEDFORWARD_UNITS), MODEL_WIDTH ** -0.5, 0.15625, ((0, 16), (2, 2)), jnp.float32)
    fc2_weight = centred(streams_of[7], (FEEDFORWARD_UNITS, N_COL, 2 * MODEL_WIDTH // N_COL), FEEDFORWARD_UNITS ** -0.5, 0.078125, ((0, 16), (1, 2)), jnp.float32)
    image_cotangent = centred(streams_of[8], (IMAGE_ROWS // 2, N_COL, 2 * MODEL_WIDTH // N_COL), 1.0, 6.0, ((0, 16), (1, 2)))
    text_cotangent = centred(streams_of[9], (TEXT_ROWS // 2, N_COL, 2 * MODEL_WIDTH // N_COL), 1.0, 6.0, ((0, 16), (1, 2)))
    return dict(image_tokens=image_tokens, text_tokens=text_tokens, conditioning=conditioning, ada_weight=ada_weight, qkv_weight=qkv_weight, proj_weight=proj_weight, fc1_weight=fc1_weight, fc2_weight=fc2_weight, image_cotangent=image_cotangent, text_cotangent=text_cotangent)


EPSILON = 1e-06
HIGHEST = lax.Precision.HIGHEST

@jax.custom_vjp
def low(v):
    return lax.optimization_barrier(v.astype(jnp.bfloat16)).astype(jnp.float32)

@jax.custom_vjp
def low_back(v):
    return v

def low_keep(v):
    return (low(v), None)

def low_pass(kept, grad):
    return (grad,)

def back_keep(v):
    return (v, None)

def back_low(kept, grad):
    return (low(grad),)
low.defvjp(low_keep, low_pass)
low_back.defvjp(back_keep, back_low)

def product(spec, first, second):
    return jnp.einsum(spec, first, second, precision=HIGHEST, preferred_element_type=jnp.float32)

def unpack_rows(packed):
    half_rows, col_count, doubled = packed.shape
    piece_width = doubled // 2
    return packed.reshape(half_rows, col_count, 2, piece_width).transpose(0, 2, 1, 3).reshape(2 * half_rows, col_count * piece_width)

def pack_rows(plain):
    number_of_lines = plain.shape[0]
    piece_width = MODEL_WIDTH // N_COL
    return plain.reshape(number_of_lines // 2, 2, N_COL, piece_width).transpose(0, 2, 1, 3).reshape(number_of_lines // 2, N_COL, 2 * piece_width)

def unpack_weight(packed, groups):
    leading = packed.shape[0]
    piece_width = packed.shape[2] // groups
    return packed.reshape(leading, N_COL, groups, piece_width).transpose(0, 2, 1, 3).reshape(leading, groups, N_COL * piece_width)

def layer_norm(values):
    average = lax.optimization_barrier(jnp.mean(values, axis=-1, keepdims=True))
    meansq = lax.optimization_barrier(jnp.mean(values * values, axis=-1, keepdims=True))
    return (values - average) * lax.rsqrt(meansq - average * average + EPSILON)

def attention(queries, key_rows, values):
    length = queries.shape[0]
    queries = queries.reshape(length, HEADS, HEAD_DIM)
    key_rows = key_rows.reshape(length, HEADS, HEAD_DIM)
    values = values.reshape(length, HEADS, HEAD_DIM)
    scores = low_back(product('qhd,khd->hqk', queries, key_rows) * HEAD_DIM ** (-0.5))
    highest = lax.optimization_barrier(jnp.max(scores, axis=-1, keepdims=True))
    expo = jnp.exp(scores - highest)
    probabilities = expo / lax.optimization_barrier(jnp.sum(expo, axis=-1, keepdims=True))
    return product('hqk,khd->qhd', low(probabilities), values).reshape(length, MODEL_WIDTH)

def block_sequence(weights, image_rows, text_rows, modulation):
    ada_low, qkv_low, proj_low, fc1_low, fc2_low = weights
    inputs = (image_rows, text_rows)
    projected = []
    for modality_label in range(2):
        hidden = low(low_back(layer_norm(inputs[modality_label]) * (1.0 + modulation[modality_label, 1]) + modulation[modality_label, 0]))
        projected.append([low(low_back(product('nd,de->ne', hidden, qkv_low[:, modality_label, column]))) for column in range(3)])
    joined = [jnp.concatenate([projected[1][column], projected[0][column]], axis=0) for column in range(3)]
    attended = low(low_back(attention(joined[0], joined[1], joined[2])))
    text_count = text_rows.shape[0]
    pieces = (attended[text_count:], attended[:text_count])
    results = []
    for modality_label in range(2):
        branch_one = low_back(product('nd,de->ne', pieces[modality_label], proj_low[:, modality_label]))
        middle = inputs[modality_label] + modulation[modality_label, 2] * branch_one
        hidden_two = low(low_back(layer_norm(middle) * (1.0 + modulation[modality_label, 4]) + modulation[modality_label, 3]))
        preact = low_back(product('nd,df->nf', hidden_two, fc1_low[:, modality_label]))
        activated = low(jax.nn.gelu(preact, approximate=True))
        latter_path = low_back(product('nf,fe->ne', activated, fc2_low[:, modality_label]))
        results.append(middle + modulation[modality_label, 5] * latter_path)
    return (results[0], results[1])

def forward(image_tokens, text_tokens, conditioning, ada_weight, qkv_weight, proj_weight, fc1_weight, fc2_weight):
    ada_plain = unpack_weight(ada_weight, 12).reshape(MODEL_WIDTH, 2, 6, MODEL_WIDTH)
    qkv_plain = unpack_weight(qkv_weight, 6).reshape(MODEL_WIDTH, 2, 3, MODEL_WIDTH)
    proj_plain = unpack_weight(proj_weight, 2)
    fc2_plain = unpack_weight(fc2_weight, 2)
    weights = (low(ada_plain), low(qkv_plain), low(proj_plain), low(fc1_weight), low(fc2_plain))
    silu_cond = low(jax.nn.silu(conditioning))
    modulation = low_back(product('sd,dtje->stje', silu_cond, weights[0]))
    images = unpack_rows(image_tokens).reshape(SEQS, IMG, MODEL_WIDTH)
    texts = unpack_rows(text_tokens).reshape(SEQS, TXT, MODEL_WIDTH)
    checked = jax.checkpoint(block_sequence)
    image_out, text_out = lax.map(lambda member: checked(weights, member[0], member[1], member[2]), (images, texts, modulation))
    return (pack_rows(image_out.reshape(SEQS * IMG, MODEL_WIDTH)), pack_rows(text_out.reshape(SEQS * TXT, MODEL_WIDTH)))

def reference(image_tokens, text_tokens, conditioning, ada_weight, qkv_weight, proj_weight, fc1_weight, fc2_weight, image_cotangent, text_cotangent):
    results, pullback = jax.vjp(forward, image_tokens.astype(jnp.float32), text_tokens.astype(jnp.float32), conditioning, ada_weight, qkv_weight, proj_weight, fc1_weight, fc2_weight)
    gradients = pullback((image_cotangent.astype(jnp.float32), text_cotangent.astype(jnp.float32)))
    return (results[0].astype(jnp.bfloat16), results[1].astype(jnp.bfloat16), gradients[0], gradients[1], gradients[2], gradients[3], gradients[4], gradients[5], gradients[6], gradients[7])
```

```python
from functools import partial

import jax
import jax.numpy as jnp
from jax import lax
from jax.sharding import PartitionSpec as P

MODEL_WIDTH = 1536
HEAD_DIM = 64
FEEDFORWARD_UNITS = 6144
EPSILON = 1e-06

bf16 = jnp.bfloat16
f32 = jnp.float32


def dot(spec, a, b):
    return jnp.einsum(spec, a, b, preferred_element_type=f32)


def attend_forward(q, k, v):
    length, width = q.shape
    heads = width // HEAD_DIM
    q = q.reshape(length, heads, HEAD_DIM)
    k = k.reshape(length, heads, HEAD_DIM)
    v = v.reshape(length, heads, HEAD_DIM)
    scores = dot("qhd,khd->hqk", q, k) * HEAD_DIM ** (-0.5)
    highest = jnp.max(scores, axis=-1, keepdims=True)
    expo = jnp.exp(scores - highest)
    totals = jnp.sum(expo, axis=-1, keepdims=True)
    probs = expo / totals
    out = dot("hqk,khd->qhd", probs.astype(bf16), v)
    return out.reshape(length, width).astype(bf16), highest + jnp.log(totals)


def attend_back(q, k, v, d_out, log_totals):
    length, width = q.shape
    heads = width // HEAD_DIM
    factor = HEAD_DIM ** (-0.5)
    q = q.reshape(length, heads, HEAD_DIM)
    k = k.reshape(length, heads, HEAD_DIM)
    v = v.reshape(length, heads, HEAD_DIM)
    d_out = d_out.reshape(length, heads, HEAD_DIM)
    scores = dot("qhd,khd->hqk", q, k) * factor
    probs = jnp.exp(scores - log_totals)
    d_v = dot("hqk,qhd->khd", probs.astype(bf16), d_out)
    d_probs = dot("qhd,khd->hqk", d_out, v)
    d_scores = (
        probs * (d_probs - jnp.sum(d_probs * probs, axis=-1, keepdims=True))
    ).astype(bf16)
    d_q = dot("hqk,khd->qhd", d_scores, k) * factor
    d_k = dot("hqk,qhd->khd", d_scores, q) * factor
    return [g.reshape(length, width).astype(bf16) for g in (d_q, d_k, d_v)]


def row_factors(rows):
    if rows % 4 == 0:
        z = 4 if rows >= 16 else 2
        return z, rows // 2 // z
    return 1, rows // 2


def per_device(
    R,
    C,
    image_tokens,
    text_tokens,
    conditioning,
    ada_weight,
    qkv_weight,
    proj_weight,
    fc1_weight,
    fc2_weight,
    image_cotangent,
    text_cotangent,
):
    w = image_tokens.shape[2] // 2
    me_r = lax.axis_index("row")
    me_c = lax.axis_index("col")
    Z, Y = row_factors(R)
    ZY = Z * Y
    my_core = me_r % 2
    my_y = (me_r // 2) % Y
    pair = C == 2
    parity = pair and (R // C) % C == 0
    CORE = [(r, r ^ 1) for r in range(R)]
    YSWAP = [(r, r ^ 2) for r in range(R)]
    YGROUPS = [[(z * Y + y) * 2 + c for y in range(Y)] for z in range(Z) for c in range(2)]
    ZGROUPS = [[(z * Y + y) * 2 + c for z in range(Z)] for y in range(Y) for c in range(2)]
    XSWAP = [(0, 1), (1, 0)]

    def swap(a):
        return lax.ppermute(a, "col", XSWAP)

    def natural(own, other, axis=-1):
        first = jnp.where(me_c == 0, own, other)
        second = jnp.where(me_c == 0, other, own)
        return jnp.concatenate([first, second], axis=axis)

    def gather_features(own):
        if pair:
            return natural(own, swap(own))
        return lax.all_gather(own, "col", axis=own.ndim - 1, tiled=True)

    def scatter_features(make):
        if pair:
            arrived = swap(make(1 - me_c).astype(bf16))
            return make(me_c) + arrived.astype(f32)
        whole = jnp.concatenate([make(c) for c in range(C)], axis=-1)
        return lax.psum_scatter(whole, "col", scatter_dimension=1, tiled=True)

    def sum_col(a):
        if pair:
            return a + swap(a)
        return lax.psum(a, "col")

    def unpack(packed):
        rows = packed.reshape(packed.shape[0], 2 * w)
        return jnp.concatenate([rows[:, :w], rows[:, w:]], axis=0)

    def pack(plain):
        half = plain.shape[0] // 2
        return jnp.concatenate([plain[:half], plain[half:]], axis=1).reshape(half, 1, 2 * w)

    def gather_rows(a):
        return lax.all_gather(a, "row", axis=0, tiled=True)

    def reduce_rows(part):
        arrived = lax.ppermute(part(1 - my_core).astype(bf16), "row", CORE)
        own = part(my_core) + arrived.astype(f32)
        blk, n = own.shape[0] // ZY, own.shape[1]
        own = own.reshape(Z, Y, blk, n)
        if Y == 2:
            sent = lax.dynamic_index_in_dim(own, 1 - my_y, 1, keepdims=False).astype(bf16)
            kept = lax.dynamic_index_in_dim(own, my_y, 1, keepdims=False)
            kept = kept + lax.ppermute(sent, "row", YSWAP).astype(f32)
        elif Y > 1:
            kept = lax.psum_scatter(
                own.astype(bf16), "row", scatter_dimension=1, axis_index_groups=YGROUPS
            )
        else:
            kept = own[:, 0]
        if Z > 1:
            kept = lax.psum_scatter(
                kept.astype(bf16), "row", scatter_dimension=0, axis_index_groups=ZGROUPS
            )
        else:
            kept = kept[0]
        return kept.astype(f32)

    def rows_of(a, core):
        t, width = a.shape
        blk = width // R
        parts = a.reshape(t, ZY, 2, blk)
        return lax.dynamic_index_in_dim(parts, core, 2, keepdims=False).reshape(t, ZY * blk)

    qkv_shard = qkv_weight.reshape(qkv_weight.shape[0], 6 * w).astype(bf16)
    proj_shard = proj_weight.reshape(proj_weight.shape[0], 2 * w).astype(bf16)
    fc1_shard = fc1_weight.astype(bf16)
    fc2_shard = fc2_weight.reshape(fc2_weight.shape[0], 2 * w).astype(bf16)
    units = fc1_shard.shape[2]
    blk2 = fc2_shard.shape[0]
    blocks = units // blk2
    ada_shard = ada_weight.reshape(ada_weight.shape[0], 12 * w).astype(bf16)

    if parity:
        TO = [(r * C + c, ((r // C) * C + c) * C + r % C) for r in range(R) for c in range(C)]
        half = blocks // 2
        group = fc1_shard.reshape(fc1_shard.shape[0], 2, half, 2, blk2)

        def fc1_swap(g):
            mine = lax.dynamic_index_in_dim(g, me_c, 3, keepdims=False)
            theirs = swap(lax.dynamic_index_in_dim(g, 1 - me_c, 3, keepdims=False))
            return natural(mine, theirs, axis=2)

        def fc1_unswap(g):
            first, second = g[:, :, :half], g[:, :, half:]
            mine = jnp.where(me_c == 0, first, second)
            theirs = swap(jnp.where(me_c == 0, second, first))
            even = jnp.where(me_c == 0, mine, theirs)
            odd = jnp.where(me_c == 0, theirs, mine)
            return jnp.stack([even, odd], axis=3)

        fc1_shard = fc1_swap(group).reshape(fc1_shard.shape)
    else:
        TO = [
            (r * C + c, (c * (R // C) + r % (R // C)) * C + r // (R // C))
            for r in range(R)
            for c in range(C)
        ]
    FROM = [(b, a) for a, b in TO]
    fc2_shard = lax.ppermute(fc2_shard, ("row", "col"), TO)

    qkv_full = [gather_rows(qkv_shard[:, m * 3 * w : (m + 1) * 3 * w]) for m in range(2)]
    proj_full = gather_rows(proj_shard)
    proj_full = [proj_full[:, m * w : (m + 1) * w] for m in range(2)]
    fc1_full = [gather_rows(fc1_shard[:, m]) for m in range(2)]
    fc2_parts = []
    for m in range(2):
        got = gather_rows(fc2_shard[:, m * w : (m + 1) * w])
        if parity:
            got = got.reshape(R // C, C, blk2, w).transpose(1, 0, 2, 3)
        fc2_parts.append(got.reshape(C, units, w))

    silu_all = lax.all_gather(jax.nn.silu(conditioning).astype(bf16), ("row", "col"), axis=0, tiled=True)
    silu_all = silu_all.reshape(-1, MODEL_WIDTH)
    ada_rows = ada_shard.shape[0]
    silu_rows = lax.dynamic_slice_in_dim(silu_all, me_r * ada_rows, ada_rows, 1)
    mod = lax.psum_scatter(
        dot("sd,de->se", silu_rows, ada_shard), "row", scatter_dimension=0, tiled=True
    ).reshape(2, 6, w)

    packed = (image_tokens, text_tokens)
    inputs = [unpack(p).astype(f32) for p in packed]
    cotangents = [unpack(p).astype(f32) for p in (image_cotangent, text_cotangent)]
    counts = [a.shape[0] for a in inputs]

    if pair:
        inputs_full = [natural(unpack(p), unpack(swap(p))).astype(f32) for p in packed]
    else:
        inputs_full = [gather_features(unpack(p)).astype(f32) for p in packed]
    first_mod = gather_features(mod[:, 0:2].reshape(4, w)).reshape(2, 2, MODEL_WIDTH)

    mean1, rstd1, hidden1 = [], [], []
    for m in range(2):
        x = inputs_full[m]
        mean = jnp.sum(x, axis=-1, keepdims=True) / MODEL_WIDTH
        meansq = jnp.sum(x * x, axis=-1, keepdims=True) / MODEL_WIDTH
        rstd = lax.rsqrt(meansq - mean * mean + EPSILON)
        mean1.append(mean)
        rstd1.append(rstd)
        hidden1.append(
            ((x - mean) * rstd * (1.0 + first_mod[m, 1]) + first_mod[m, 0]).astype(bf16)
        )
    norm1 = [(inputs[m] - mean1[m]) * rstd1[m] for m in range(2)]

    d_branch2 = [(mod[m, 5] * cotangents[m]).astype(bf16) for m in range(2)]
    d_branch2_full = [gather_features(d_branch2[m]) for m in range(2)]

    projected = [dot("td,de->te", hidden1[m], qkv_full[m]).astype(bf16) for m in range(2)]
    joined = jnp.concatenate(projected, axis=0)
    q, k, v = (joined[:, j * w : (j + 1) * w] for j in range(3))
    attended, log_totals = attend_forward(q, k, v)
    attended = [attended[: counts[0]], attended[counts[0] :]]
    attended_full = [gather_features(a) for a in attended]
    branch1 = [dot("te,eb->tb", attended_full[m], proj_full[m]) for m in range(2)]
    middle = [inputs[m] + mod[m, 2] * branch1[m] for m in range(2)]

    def token_sums(firsts, seconds):
        own = jnp.concatenate(
            [
                jnp.stack([jnp.sum(firsts[m], axis=-1), jnp.sum(seconds[m], axis=-1)])
                for m in range(2)
            ],
            axis=1,
        )
        both = sum_col(own) / MODEL_WIDTH
        parts = (both[:, : counts[0]], both[:, counts[0] :])
        return [(p[0][:, None], p[1][:, None]) for p in parts]

    stats = token_sums(middle, [a * a for a in middle])
    rstd2 = [lax.rsqrt(sq - mean * mean + EPSILON) for mean, sq in stats]
    norm2 = [(middle[m] - stats[m][0]) * rstd2[m] for m in range(2)]
    hidden2 = [(norm2[m] * (1.0 + mod[m, 4]) + mod[m, 3]).astype(bf16) for m in range(2)]
    hidden2_full = [gather_features(a) for a in hidden2]
    preact = [dot("td,df->tf", hidden2_full[m], fc1_full[m]) for m in range(2)]
    activated = [jax.nn.gelu(a, approximate=True).astype(bf16) for a in preact]

    def fc2_block(m, c):
        return lax.dynamic_index_in_dim(fc2_parts[m], c, 0, keepdims=False)

    branch2 = [
        scatter_features(lambda c, m=m: dot("tf,fe->te", activated[m], fc2_block(m, c)))
        for m in range(2)
    ]
    results = [middle[m] + mod[m, 5] * branch2[m] for m in range(2)]
    d_gate2 = [jnp.sum(cotangents[m] * branch2[m], axis=0) for m in range(2)]

    d_activated = [
        dot("tce,cfe->tf", d_branch2_full[m].reshape(-1, C, w), fc2_parts[m]) for m in range(2)
    ]
    d_preact = []
    for m in range(2):
        _, pullback = jax.vjp(partial(jax.nn.gelu, approximate=True), preact[m])
        d_preact.append(pullback(d_activated[m])[0].astype(bf16))
    d_hidden2 = [
        scatter_features(
            lambda c, m=m: dot(
                "tf,df->td", d_preact[m], lax.dynamic_slice_in_dim(fc1_full[m], c * w, w, 0)
            )
        )
        .astype(bf16)
        .astype(f32)
        for m in range(2)
    ]

    def fc2_part(m):
        def part(core):
            if parity:
                grad = lax.dynamic_slice_in_dim(d_branch2_full[m], core * w, w, 1)
                return dot("tf,te->fe", activated[m], grad)
            whole = jnp.concatenate(
                [
                    dot("tf,te->fe", activated[m], d_branch2_full[m][:, c * w : (c + 1) * w])
                    for c in range(C)
                ],
                axis=0,
            )
            return lax.dynamic_index_in_dim(
                whole.reshape(ZY, 2, blk2, w), core, 1, keepdims=False
            ).reshape(ZY * blk2, w)

        return part

    grad_fc2 = jnp.concatenate([reduce_rows(fc2_part(m)) for m in range(2)], axis=1)
    grad_fc2 = lax.ppermute(grad_fc2, ("row", "col"), FROM)

    def product_part(a, b):
        return lambda core: dot("tp,tn->pn", rows_of(a, core), b)

    grad_fc1 = jnp.stack(
        [reduce_rows(product_part(hidden2_full[m], d_preact[m])) for m in range(2)], axis=1
    )
    if parity:
        grad_fc1 = fc1_unswap(grad_fc1.reshape(-1, 2, blocks, blk2)).reshape(grad_fc1.shape)

    d_shift2 = [jnp.sum(d_hidden2[m], axis=0) for m in range(2)]
    d_scale2 = [jnp.sum(d_hidden2[m] * norm2[m], axis=0) for m in range(2)]

    def norm_back(d_hidden, norm, rstd, scale):
        d_norm = [d_hidden[m] * (1.0 + scale[m]) for m in range(2)]
        sums = token_sums(d_norm, [d_norm[m] * norm[m] for m in range(2)])
        return [rstd[m] * (d_norm[m] - sums[m][0] - norm[m] * sums[m][1]) for m in range(2)]

    back2 = norm_back(d_hidden2, norm2, rstd2, [mod[m, 4] for m in range(2)])
    d_middle = [cotangents[m] + back2[m] for m in range(2)]
    d_branch1 = [(mod[m, 2] * d_middle[m]).astype(bf16) for m in range(2)]
    d_gate1 = [jnp.sum(d_middle[m] * branch1[m], axis=0) for m in range(2)]

    d_attended = [
        scatter_features(
            lambda c, m=m: dot(
                "tv,yv->ty", d_branch1[m], lax.dynamic_slice_in_dim(proj_full[m], c * w, w, 0)
            )
        ).astype(bf16)
        for m in range(2)
    ]
    grad_proj = jnp.concatenate(
        [reduce_rows(product_part(attended_full[m], d_branch1[m])) for m in range(2)], axis=1
    )
    d_joined = jnp.concatenate(
        attend_back(q, k, v, jnp.concatenate(d_attended, axis=0), log_totals), axis=1
    )
    d_projected = [d_joined[: counts[0]], d_joined[counts[0] :]]
    d_hidden1 = [
        scatter_features(
            lambda c, m=m: dot(
                "te,de->td", d_projected[m], lax.dynamic_slice_in_dim(qkv_full[m], c * w, w, 0)
            )
        )
        .astype(bf16)
        .astype(f32)
        for m in range(2)
    ]
    grad_qkv = jnp.concatenate(
        [reduce_rows(product_part(hidden1[m], d_projected[m])) for m in range(2)], axis=1
    )
    d_shift1 = [jnp.sum(d_hidden1[m], axis=0) for m in range(2)]
    d_scale1 = [jnp.sum(d_hidden1[m] * norm1[m], axis=0) for m in range(2)]
    back1 = norm_back(d_hidden1, norm1, rstd1, [mod[m, 1] for m in range(2)])
    grad_inputs = [d_middle[m] + back1[m] for m in range(2)]

    d_mod = jnp.concatenate(
        [
            part[m].reshape(1, w)
            for m in range(2)
            for part in (d_shift1, d_scale1, d_gate1, d_shift2, d_scale2, d_gate2)
        ],
        axis=1,
    ).astype(bf16)
    d_mod_all = gather_rows(d_mod)
    grad_ada = dot("sd,se->de", silu_rows, d_mod_all)
    d_silu_part = dot("se,de->sd", d_mod_all, ada_shard)
    d_silu = lax.all_to_all(d_silu_part, "row", 0, 0, tiled=True).reshape(1, MODEL_WIDTH)
    d_silu = lax.psum_scatter(d_silu, "col", scatter_dimension=1, tiled=True)
    _, pullback = jax.vjp(jax.nn.silu, conditioning)
    grad_cond = pullback(d_silu)[0]

    def stored(gradient):
        return gradient.reshape(gradient.shape[0], 1, -1)

    return (
        pack(results[0]).astype(bf16),
        pack(results[1]).astype(bf16),
        pack(grad_inputs[0]),
        pack(grad_inputs[1]),
        grad_cond,
        stored(grad_ada),
        stored(grad_qkv),
        stored(grad_proj),
        grad_fc1,
        stored(grad_fc2),
    )


def solution(mesh):
    tokens = P("row", "col", None)
    units = P("row", None, "col")
    cond = P("row", "col")
    return jax.shard_map(
        partial(per_device, mesh.shape["row"], mesh.shape["col"]),
        mesh=mesh,
        in_specs=(tokens, tokens, cond, tokens, tokens, tokens, units, tokens, tokens, tokens),
        out_specs=(tokens, tokens, tokens, tokens, cond, tokens, tokens, tokens, units, tokens),
        check_vma=False,
    )
```

```python
from functools import partial

import jax
import jax.numpy as jnp
from jax import lax
from jax.experimental import pallas as pl
from jax.experimental.pallas import tpu as pltpu
from jax.sharding import PartitionSpec as P

MODEL_WIDTH = 1536
HEAD_DIM = 64
FEEDFORWARD_UNITS = 6144
EPSILON = 1e-06
PAIR = 2 * HEAD_DIM
BLOCK = 256
MASKED = -1e30

bf16 = jnp.bfloat16
f32 = jnp.float32


def dot(spec, a, b):
    return jnp.einsum(spec, a, b, preferred_element_type=f32)


def mm_nn(a, b):
    return lax.dot_general(a, b, (((1,), (0,)), ((), ())), preferred_element_type=f32)


def mm_nt(a, b):
    return lax.dot_general(a, b, (((1,), (1,)), ((), ())), preferred_element_type=f32)


def attend_kernel(real, qi, qt, ki, kt, vi, vt, oi, ot, lse, q_s, k_s, v_s, s_0, s_1):
    ni, n = qi.shape[0], q_s.shape[0]
    scale = jnp.asarray(HEAD_DIM**-0.5, bf16)
    q_s[:ni, :] = qi[...] * scale
    q_s[ni:, :] = qt[...] * scale
    k_s[:ni, :] = ki[...]
    k_s[ni:, :] = kt[...]
    v_s[:, :ni] = vi[...].T
    v_s[:, ni:] = vt[...].T
    key = lax.broadcasted_iota(jnp.int32, (n - ni, BLOCK), 0)
    held = (s_0, s_1)

    def scores(i, h):
        head = slice(h * HEAD_DIM, (h + 1) * HEAD_DIM)
        held[h][...] = mm_nt(k_s[:, head], q_s[i * BLOCK : (i + 1) * BLOCK, head])

    def mix(i, h):
        head = slice(h * HEAD_DIM, (h + 1) * HEAD_DIM)
        s = held[h][...]
        s_i, s_t = s[:ni], jnp.where(key < real, s[ni:], MASKED)
        top = jnp.maximum(
            jnp.max(s_i, axis=0, keepdims=True), jnp.max(s_t, axis=0, keepdims=True)
        )
        e_i, e_t = jnp.exp(s_i - top), jnp.exp(s_t - top)
        total = jnp.sum(e_i, axis=0, keepdims=True) + jnp.sum(e_t, axis=0, keepdims=True)
        part = 1.0 / total
        lse[0, h : h + 1, i * BLOCK : (i + 1) * BLOCK] = top + jnp.log(total)
        return mm_nn(v_s[head, :ni], (e_i * part).astype(bf16)) + mm_nn(
            v_s[head, ni:], (e_t * part).astype(bf16)
        )

    blocks = n // BLOCK
    scores(0, 0)
    for i in range(blocks):
        scores(i, 1)
        first = mix(i, 0)
        if i + 1 < blocks:
            scores(i + 1, 0)
        out = jnp.concatenate([first, mix(i, 1)], axis=0).T.astype(bf16)
        if i * BLOCK < ni:
            oi[i * BLOCK : (i + 1) * BLOCK, :] = out
        else:
            ot[i * BLOCK - ni : (i + 1) * BLOCK - ni, :] = out


def attend_back_kernel(
    real, qi, qt, ki, kt, vi, vt, di, dt, lse, dqi, dqt, dki, dkt, dvi, dvt,
    q_s, k_s, kt_s, v_s, d_s, dq_s, dk_s, dv_s,
):
    ni, n = qi.shape[0], q_s.shape[0]
    scale = HEAD_DIM**-0.5
    q_s[:ni, :] = qi[...] * jnp.asarray(scale, bf16)
    q_s[ni:, :] = qt[...] * jnp.asarray(scale, bf16)
    k_s[:ni, :] = ki[...]
    k_s[ni:, :] = kt[...]
    kt_s[:, :ni] = ki[...].T
    kt_s[:, ni:] = kt[...].T
    v_s[:ni, :] = vi[...]
    v_s[ni:, :] = vt[...]
    d_s[:ni, :] = di[...]
    d_s[ni:, :] = dt[...]
    key = lax.broadcasted_iota(jnp.int32, (n - ni, BLOCK), 0)
    for i in range(n // BLOCK):
        rows = slice(i * BLOCK, (i + 1) * BLOCK)
        dq = []
        for h in range(2):
            head = slice(h * HEAD_DIM, (h + 1) * HEAD_DIM)
            q, d = q_s[rows, head], d_s[rows, head]
            s = mm_nt(k_s[:, head], q)
            s = jnp.concatenate([s[:ni], jnp.where(key < real, s[ni:], MASKED)], axis=0)
            p = jnp.exp(s - lse[0, h : h + 1, rows])
            t = p * mm_nt(v_s[:, head], d)
            d_scores = (t - p * jnp.sum(t, axis=0, keepdims=True)).astype(bf16)
            dv, dk = mm_nn(p.astype(bf16), d), mm_nn(d_scores, q)
            if i == 0:
                dv_s[:, head] = dv
                dk_s[:, head] = dk
            else:
                dv_s[:, head] += dv
                dk_s[:, head] += dk
            dq.append(mm_nn(kt_s[head, :], d_scores))
        dq_s[:, rows] = jnp.concatenate(dq, axis=0)
    d_q = (dq_s[...] * scale).T.astype(bf16)
    dqi[...] = d_q[:ni]
    dqt[...] = d_q[ni:]
    dki[...] = dk_s[:ni, :].astype(bf16)
    dkt[...] = dk_s[ni:, :].astype(bf16)
    dvi[...] = dv_s[:ni, :].astype(bf16)
    dvt[...] = dv_s[ni:, :].astype(bf16)


def projection_specs(ni, nt, total, first):
    specs = []
    for j in range(3):
        at = lambda p, j=j: (0, j * total + first + p)
        specs += [pl.BlockSpec((ni, PAIR), at), pl.BlockSpec((nt, PAIR), at)]
    return specs


def attend(image, text, real, first, pairs):
    ni, nt = image.shape[0], text.shape[0]
    n, total = ni + nt, image.shape[1] // 3 // PAIR
    at = lambda p: (0, p)
    return pl.pallas_call(
        partial(attend_kernel, real),
        grid=(pairs,),
        in_specs=projection_specs(ni, nt, total, first),
        out_specs=[
            pl.BlockSpec((ni, PAIR), at),
            pl.BlockSpec((nt, PAIR), at),
            pl.BlockSpec((1, 2, n), lambda p: (p, 0, 0)),
        ],
        out_shape=[
            jax.ShapeDtypeStruct((ni, pairs * PAIR), bf16),
            jax.ShapeDtypeStruct((nt, pairs * PAIR), bf16),
            jax.ShapeDtypeStruct((pairs, 2, n), f32),
        ],
        scratch_shapes=[
            pltpu.VMEM((n, PAIR), bf16),
            pltpu.VMEM((n, PAIR), bf16),
            pltpu.VMEM((PAIR, n), bf16),
            pltpu.VMEM((n, BLOCK), f32),
            pltpu.VMEM((n, BLOCK), f32),
        ],
        compiler_params=pltpu.CompilerParams(vmem_limit_bytes=40 * 2**20),
        cost_estimate=pl.CostEstimate(
            flops=pairs * 2 * n * n * 256 * 2 * 2,
            bytes_accessed=pairs * n * PAIR * 2 * 4,
            transcendentals=pairs * 2 * n * n,
        ),
    )(image, text, image, text, image, text)


def attend_back(image, text, real, first, pairs, d_image, d_text, lse):
    ni, nt = image.shape[0], text.shape[0]
    n, total = ni + nt, image.shape[1] // 3 // PAIR
    at = lambda p: (0, p)
    one_i, one_t = pl.BlockSpec((ni, PAIR), at), pl.BlockSpec((nt, PAIR), at)
    out_i = jax.ShapeDtypeStruct((ni, pairs * PAIR), bf16)
    out_t = jax.ShapeDtypeStruct((nt, pairs * PAIR), bf16)
    return pl.pallas_call(
        partial(attend_back_kernel, real),
        grid=(pairs,),
        in_specs=projection_specs(ni, nt, total, first)
        + [one_i, one_t, pl.BlockSpec((1, 2, n), lambda p: (p, 0, 0))],
        out_specs=[one_i, one_t] * 3,
        out_shape=[out_i, out_t] * 3,
        scratch_shapes=[
            pltpu.VMEM((n, PAIR), bf16),
            pltpu.VMEM((n, PAIR), bf16),
            pltpu.VMEM((PAIR, n), bf16),
            pltpu.VMEM((n, PAIR), bf16),
            pltpu.VMEM((n, PAIR), bf16),
            pltpu.VMEM((PAIR, n), f32),
            pltpu.VMEM((n, PAIR), f32),
            pltpu.VMEM((n, PAIR), f32),
        ],
        compiler_params=pltpu.CompilerParams(vmem_limit_bytes=40 * 2**20),
        cost_estimate=pl.CostEstimate(
            flops=pairs * 2 * n * n * 256 * 2 * 5,
            bytes_accessed=pairs * n * PAIR * 2 * 8,
            transcendentals=pairs * 2 * n * n,
        ),
    )(image, text, image, text, image, text, d_image, d_text, lse)


def split_heads(a):
    return a.reshape(a.shape[0], -1, HEAD_DIM)


def plain_attend(image, text, real):
    joined = jnp.concatenate([image, text[:real]], axis=0)
    q, k, v = (split_heads(a) for a in jnp.split(joined, 3, axis=1))
    scores = dot("qhd,khd->hqk", q, k) * HEAD_DIM ** (-0.5)
    top = jnp.max(scores, axis=-1, keepdims=True)
    expo = jnp.exp(scores - top)
    total = jnp.sum(expo, axis=-1, keepdims=True)
    out = dot("hqk,khd->qhd", (expo / total).astype(bf16), v).astype(bf16)
    out = out.reshape(joined.shape[0], -1)
    pad = ((0, text.shape[0] - real), (0, 0))
    ni = image.shape[0]
    return out[:ni], jnp.pad(out[ni:], pad), top + jnp.log(total)


def plain_attend_back(image, text, real, d_image, d_text, lse):
    ni, width = image.shape[0], d_image.shape[1]
    joined = jnp.concatenate([image, text[:real]], axis=0)
    q, k, v = (split_heads(a) for a in jnp.split(joined, 3, axis=1))
    d = split_heads(jnp.concatenate([d_image, d_text[:real]], axis=0))
    factor = HEAD_DIM ** (-0.5)
    probs = jnp.exp(dot("qhd,khd->hqk", q, k) * factor - lse)
    d_v = dot("hqk,qhd->khd", probs.astype(bf16), d)
    d_probs = dot("qhd,khd->hqk", d, v)
    d_scores = probs * (d_probs - jnp.sum(d_probs * probs, axis=-1, keepdims=True))
    d_scores = d_scores.astype(bf16)
    d_q = dot("hqk,khd->qhd", d_scores, k) * factor
    d_k = dot("hqk,qhd->khd", d_scores, q) * factor
    outs = []
    for g in (d_q, d_k, d_v):
        g = g.reshape(-1, width).astype(bf16)
        outs += [g[:ni], jnp.pad(g[ni:], ((0, text.shape[0] - real), (0, 0)))]
    return outs


def gelu_both(v):
    root = (2.0 / jnp.pi) ** 0.5
    t = jnp.tanh(root * (v + 0.044715 * (v * v * v)))
    half = 0.5 * (1.0 + t)
    slope = half + 0.5 * v * (1.0 - t * t) * (root * (1.0 + 3.0 * 0.044715 * (v * v)))
    return v * half, slope


def row_factors(rows):
    if rows % 4 == 0:
        z = 4 if rows >= 16 else 2
        return z, rows // 2 // z
    return 1, rows // 2


def after(value, *earlier):
    return lax.optimization_barrier((value, *earlier))[0]


def per_device(
    R,
    C,
    image_tokens,
    text_tokens,
    conditioning,
    ada_weight,
    qkv_weight,
    proj_weight,
    fc1_weight,
    fc2_weight,
    image_cotangent,
    text_cotangent,
):
    w = image_tokens.shape[2] // 2
    me_r = lax.axis_index("row")
    me_c = lax.axis_index("col")
    Z, Y = row_factors(R)
    ZY = Z * Y
    my_core = me_r % 2
    my_y = (me_r // 2) % Y
    pair = C == 2
    parity = pair and (R // C) % C == 0
    kernels = w % PAIR == 0
    both = range(2)
    CORE = [(r, r ^ 1) for r in range(R)]
    YSWAP = [(r, r ^ 2) for r in range(R)]
    YGROUPS = [[(z * Y + y) * 2 + c for y in range(Y)] for z in range(Z) for c in range(2)]
    ZGROUPS = [[(z * Y + y) * 2 + c for z in range(Z)] for y in range(Y) for c in range(2)]
    XSWAP = [(0, 1), (1, 0)]

    def swap(a):
        return lax.ppermute(a, "col", XSWAP)

    def natural(own, other, axis=-1):
        first = jnp.where(me_c == 0, own, other)
        second = jnp.where(me_c == 0, other, own)
        return jnp.concatenate([first, second], axis=axis)

    def send(own):
        if pair:
            return swap(own)
        return lax.all_gather(own, "col", axis=own.ndim - 1, tiled=True)

    def whole(own, got):
        return natural(own, got) if pair else got

    def gather_features(own):
        return whole(own, send(own))

    def col_start(makes):
        if pair:
            sent = jnp.concatenate([make(1 - me_c).astype(bf16) for make in makes], axis=0)
            return sent, swap(sent)
        sent = jnp.concatenate(
            [jnp.concatenate([make(c) for c in range(C)], axis=-1) for make in makes], axis=0
        )
        return sent, lax.psum_scatter(sent, "col", scatter_dimension=1, tiled=True)

    def col_end(makes, state, *earlier):
        got = after(state[1], *earlier)
        parts = (got[: counts[0]].astype(f32), got[counts[0] :].astype(f32))
        return [make(me_c) + part if pair else part for make, part in zip(makes, parts)]

    def sum_col(a):
        return lax.psum(a, "col")

    def core_start(part):
        sent = part(1 - my_core).astype(bf16)
        return sent, lax.ppermute(sent, "row", CORE)

    def y_start(parts, gots):
        owns = []
        for part, got in zip(parts, gots):
            own = part(my_core) + got.astype(f32)
            owns.append(own.reshape(Z, Y, own.shape[0] // ZY, own.shape[1]))
        if Y == 2:
            sent = jnp.concatenate(
                [
                    lax.dynamic_index_in_dim(own, 1 - my_y, 1, keepdims=False).astype(bf16)
                    for own in owns
                ],
                axis=2,
            )
            kept = [lax.dynamic_index_in_dim(own, my_y, 1, keepdims=False) for own in owns]
            sent, *kept = lax.optimization_barrier((sent, *kept))
            return sent, kept, lax.ppermute(sent, "row", YSWAP)
        own = jnp.concatenate([own.astype(bf16) for own in owns], axis=3)
        if Y > 1:
            own = lax.psum_scatter(own, "row", scatter_dimension=1, axis_index_groups=YGROUPS)
            return own, own, None
        return own[:, 0], own[:, 0], None

    def z_start(states, previous, *earlier):
        pieces = []
        for _, kept, got in states:
            if got is None:
                pieces.append(kept.astype(bf16))
                continue
            got, at = after(got, *earlier), 0
            for k in kept:
                pieces.append((k + got[:, :, at : at + k.shape[2]].astype(f32)).astype(bf16))
                at += k.shape[2]
        kept = jnp.concatenate(pieces, axis=2)
        if Z == 1:
            return [kept, kept[0]]
        if previous is not None:
            kept, previous[1] = lax.optimization_barrier((kept, previous[1]))
        summed = lax.psum_scatter(kept, "row", scatter_dimension=0, axis_index_groups=ZGROUPS)
        return [kept, summed]

    def rows_of(a):
        t, width = a.shape
        parts = a.reshape(t, ZY, 2, width // R)
        return [
            lax.dynamic_index_in_dim(parts, core, 2, keepdims=False).reshape(t, width // 2)
            for core in (1 - my_core, my_core)
        ]

    def product_part(rows, b):
        return lambda core: dot("tp,tn->pn", rows[0] if core is not my_core else rows[1], b)

    def unpack(packed):
        rows = packed.reshape(packed.shape[0], 2 * w)
        return jnp.concatenate([rows[:, :w], rows[:, w:]], axis=0)

    def pack(plain):
        half = plain.shape[0] // 2
        return jnp.concatenate([plain[:half], plain[half:]], axis=1).reshape(half, 1, 2 * w)

    def gather_rows(a, order=None):
        return lax.all_gather(a, "row", axis=1, tiled=True, axis_index_groups=order)

    fan = MODEL_WIDTH // R
    qkv_shard = qkv_weight.reshape(fan, 6 * w)
    proj_shard = proj_weight.reshape(fan, 2 * w)
    first_shard = jnp.stack(
        [
            jnp.concatenate(
                [
                    qkv_shard[:, m * 3 * w : (m + 1) * 3 * w].astype(bf16),
                    proj_shard[:, m * w : (m + 1) * w].astype(bf16),
                ],
                axis=1,
            )
            for m in both
        ]
    )
    first_full = gather_rows(first_shard)
    qkv_full = [first_full[m, :, : 3 * w] for m in both]
    proj_full = [first_full[m, :, 3 * w :] for m in both]

    silu_own = jax.nn.silu(conditioning).astype(bf16).reshape(R // C, 1, fan)
    silu_sent = jnp.broadcast_to(silu_own[None], (C, R // C, C, fan)).reshape(R * C, fan)
    silu_got = lax.all_to_all(silu_sent, ("row", "col"), 0, 0, tiled=True).reshape(R, C, fan)
    silu_rows = lax.dynamic_index_in_dim(silu_got, me_r // (R // C), 1, keepdims=False)
    ada_shard = ada_weight.reshape(fan, 12 * w).astype(bf16)
    mod = lax.all_to_all(dot("sd,de->se", silu_rows, ada_shard), "row", 0, 0, tiled=True)
    mod = jnp.sum(mod, axis=0).reshape(2, 6, w)

    packed = (image_tokens, text_tokens)
    packed_got = [send(after(p, silu_got)) if pair else None for p in packed]
    first_mod = gather_features(mod[:, 0:2].reshape(4, w)).reshape(2, 2, MODEL_WIDTH)
    inputs = [unpack(p).astype(f32) for p in packed]
    cotangents = [unpack(p).astype(f32) for p in (image_cotangent, text_cotangent)]
    counts = [a.shape[0] for a in inputs]
    real = counts[1]
    padding = -(counts[0] + real) % BLOCK
    d_branch2 = [(mod[m, 5] * cotangents[m]).astype(bf16) for m in both]

    early = [p for p in packed_got if p is not None] + [first_mod]
    fc1_weight, fc2_weight = lax.optimization_barrier((fc1_weight, fc2_weight, *early))[:2]
    fc1_shard = jnp.stack([fc1_weight[:, m] for m in both]).astype(bf16)
    blk2 = fc2_weight.shape[0]
    fc2_shard = fc2_weight.reshape(blk2, 2 * w)
    fc2_shard = jnp.stack([fc2_shard[:, m * w : (m + 1) * w] for m in both]).astype(bf16)
    units = fc1_shard.shape[2]
    blocks = units // blk2

    if parity:
        half = blocks // 2
        MOVES = [(r * C + c, ((r // C) * C + c) * C + r % C) for r in range(R) for c in range(C)]
        MOVES = [(a, b) for a, b in MOVES if a != b]
        stays = me_r % C == me_c
        ORDER = [[k * C + c for c in range(C) for k in range(R // C)]]

        def move_units(a):
            return jnp.where(stays, a, lax.ppermute(a, ("row", "col"), MOVES))

        unmove_units = move_units
        group = fc1_shard.reshape(2, fan, half, 2, blk2)
        mine = lax.dynamic_index_in_dim(group, me_c, 3, keepdims=False)
        theirs = swap(lax.dynamic_index_in_dim(group, 1 - me_c, 3, keepdims=False))
        fc1_shard = natural(mine, theirs, axis=2).reshape(fc1_shard.shape)

        def unmove_columns(g):
            g = g.reshape(fan, 2, blocks, blk2)
            first, second = g[:, :, :half], g[:, :, half:]
            mine = jnp.where(me_c == 0, first, second)
            theirs = swap(jnp.where(me_c == 0, second, first))
            even = jnp.where(me_c == 0, mine, theirs)
            odd = jnp.where(me_c == 0, theirs, mine)
            return jnp.stack([even, odd], axis=3).reshape(fan, 2, units)

    else:
        MOVES = [
            (r * C + c, (c * (R // C) + r % (R // C)) * C + r // (R // C))
            for r in range(R)
            for c in range(C)
        ]
        ORDER = None

        def move_units(a):
            return lax.ppermute(a, ("row", "col"), MOVES)

        def unmove_units(a):
            return lax.ppermute(a, ("row", "col"), [(b, a) for a, b in MOVES])

        def unmove_columns(g):
            return g

    fc2_shard = move_units(fc2_shard)
    d_branch2_got = [send(after(d_branch2[m], fc1_shard, fc2_shard)) for m in both]
    fc1_full = gather_rows(fc1_shard)
    fc2_full = gather_rows(fc2_shard, ORDER).reshape(2, C, units, w)

    def padded(a):
        return jnp.pad(a, ((0, padding), (0, 0)))

    if pair:
        inputs_full = [natural(unpack(packed[m]), unpack(packed_got[m])) for m in both]
    else:
        inputs_full = [gather_features(unpack(p)) for p in packed]

    mean1, rstd1, hidden1 = [], [], []
    for m in both:
        x = inputs_full[m].astype(f32)
        mean = jnp.sum(x, axis=-1, keepdims=True) / MODEL_WIDTH
        meansq = jnp.sum(x * x, axis=-1, keepdims=True) / MODEL_WIDTH
        rstd = lax.rsqrt(meansq - mean * mean + EPSILON)
        mean1.append(mean)
        rstd1.append(rstd)
        hidden1.append(
            ((x - mean) * rstd * (1.0 + first_mod[m, 1]) + first_mod[m, 0]).astype(bf16)
        )
    hidden1[1] = padded(hidden1[1])
    norm1 = [(inputs[m] - mean1[m]) * rstd1[m] for m in both]
    projected = [dot("td,de->te", hidden1[m], qkv_full[m]).astype(bf16) for m in both]

    total = w // PAIR
    groups = (3 if total % 3 == 0 else 1) if kernels else 1
    pairs = total // groups
    wide = w // groups
    attended, attended_got, lse = [], [], []
    for g in range(groups):
        text = projected[1]
        if g > 1:
            text = after(text, attended_got[g - 2])
        if kernels:
            out_i, out_t, saved = attend(projected[0], text, real, g * pairs, pairs)
        else:
            out_i, out_t, saved = plain_attend(projected[0], text, real)
        attended.append(jnp.concatenate([out_i, out_t[:real]], axis=0))
        attended_got.append(send(attended[g]))
        lse.append(saved)
    attended_full = whole(
        jnp.concatenate(attended, axis=1), jnp.concatenate(attended_got, axis=1)
    )
    attended_full = [attended_full[: counts[0]], attended_full[counts[0] :]]
    attended_rows = [rows_of(a) for a in attended_full]
    hidden1_rows = [rows_of(a) for a in hidden1]
    d_branch2_full = [
        whole(d_branch2[m], after(d_branch2_got[m], attended[-1])) for m in both
    ]

    branch1 = [dot("te,eb->tb", attended_full[m], proj_full[m]) for m in both]
    middle = [inputs[m] + mod[m, 2] * branch1[m] for m in both]

    def token_sums(firsts, seconds):
        own = jnp.concatenate(
            [
                jnp.stack([jnp.sum(firsts[m], axis=-1), jnp.sum(seconds[m], axis=-1)])
                for m in both
            ],
            axis=1,
        )
        sums = sum_col(own) / MODEL_WIDTH
        parts = (sums[:, : counts[0]], sums[:, counts[0] :])
        return [(p[0][:, None], p[1][:, None]) for p in parts]

    stats = token_sums(middle, [a * a for a in middle])
    rstd2 = [lax.rsqrt(sq - mean * mean + EPSILON) for mean, sq in stats]
    norm2 = [(middle[m] - stats[m][0]) * rstd2[m] for m in both]
    hidden2 = [(norm2[m] * (1.0 + mod[m, 4]) + mod[m, 3]).astype(bf16) for m in both]
    hidden2_got = [send(a) for a in hidden2]
    hidden2_got[0], *rows = lax.optimization_barrier(
        (hidden2_got[0], *attended_rows[0], *attended_rows[1], *hidden1_rows[0], *hidden1_rows[1])
    )
    attended_rows, hidden1_rows = [rows[:2], rows[2:4]], [rows[4:6], rows[6:]]
    hidden2_full = [whole(a, got) for a, got in zip(hidden2, hidden2_got)]
    hidden2_rows = [rows_of(a) for a in hidden2_full]
    preact = [dot("td,df->tf", hidden2_full[m], fc1_full[m]) for m in both]
    pairs_of = [gelu_both(a) for a in preact]
    activated = [a.astype(bf16) for a, _ in pairs_of]
    slope = [s for _, s in pairs_of]

    def fc2_part(m, act):
        def part(core):
            if parity:
                grad = lax.dynamic_slice_in_dim(d_branch2_full[m], core * w, w, 1)
                return dot("tf,te->fe", act, grad)
            whole_grad = jnp.concatenate(
                [
                    dot("tf,te->fe", act, d_branch2_full[m][:, c * w : (c + 1) * w])
                    for c in range(C)
                ],
                axis=0,
            )
            return lax.dynamic_index_in_dim(
                whole_grad.reshape(ZY, 2, blk2, w), core, 1, keepdims=False
            ).reshape(ZY * blk2, w)

        return part

    fc2_core = [core_start(fc2_part(m, activated[m])) for m in both]
    act_later = [after(activated[m], fc2_core[0][0], fc2_core[1][0]) for m in both]
    fc2_y = y_start([fc2_part(m, act_later[m]) for m in both], [s[1] for s in fc2_core])

    grads = [after(d_branch2_full[m], fc2_y[0]) for m in both]
    none = jnp.minimum(me_r, 0)
    d_activated = [
        dot(
            "tce,cfe->tf",
            grads[m].reshape(-1, C, w),
            lax.dynamic_slice(fc2_full, (m + none, 0, 0, 0), (1, C, units, w))[0],
        )
        for m in both
    ]
    d_preact = [(d_activated[m] * slope[m]).astype(bf16) for m in both]

    def hidden2_make(m, d):
        return lambda c: dot(
            "tf,df->td", d, lax.dynamic_slice(fc1_full, (m, c * w, 0), (1, w, units))[0]
        )

    hidden2_col = col_start([hidden2_make(m, d_preact[m]) for m in both])

    def branch2_make(m, act):
        return lambda c: dot(
            "tf,fe->te", act, lax.dynamic_slice(fc2_full, (m, c, 0, 0), (1, 1, units, w))[0, 0]
        )

    act_last = [after(activated[m], hidden2_col[0]) for m in both]
    branch2_col = col_start([branch2_make(m, act_last[m]) for m in both])
    d_next = [after(d_preact[m], hidden2_col[0]) for m in both]
    fc1_core = [core_start(product_part(hidden2_rows[m], d_next[m])) for m in both]
    d_next = [after(d_next[m], fc1_core[0][0], fc1_core[1][0]) for m in both]
    fc1_y = y_start(
        [product_part(hidden2_rows[m], d_next[m]) for m in both], [s[1] for s in fc1_core]
    )
    d_next = [after(d_next[m], fc1_y[0]) for m in both]
    d_hidden2 = col_end(
        [hidden2_make(m, d_next[m]) for m in both], hidden2_col, fc1_y[0], branch2_col[0]
    )
    d_hidden2 = [d.astype(bf16) for d in d_hidden2]
    fc2_z = z_start([fc2_y], None, *d_hidden2)
    d_hidden2 = [d.astype(f32) for d in d_hidden2]

    def norm_back(d_hidden, norm, rstd, scale):
        d_norm = [d_hidden[m] * (1.0 + scale[m]) for m in both]
        sums = token_sums(d_norm, [d_norm[m] * norm[m] for m in both])
        return [rstd[m] * (d_norm[m] - sums[m][0] - norm[m] * sums[m][1]) for m in both]

    back2 = norm_back(d_hidden2, norm2, rstd2, [mod[m, 4] for m in both])
    d_middle = [cotangents[m] + back2[m] for m in both]
    d_branch1 = [(mod[m, 2] * d_middle[m]).astype(bf16) for m in both]

    def attended_make(m, g, d):
        return lambda c: dot(
            "tv,yv->ty",
            d,
            lax.dynamic_slice(first_full, (m, c * w + g * wide, 3 * w), (1, wide, w))[0],
        )

    attended_col = [
        col_start([attended_make(m, g, d_branch1[m]) for m in both]) for g in range(groups)
    ]
    sent = [state[0] for state in attended_col]
    d_last = [after(d_branch1[m], *sent) for m in both]
    proj_core = [core_start(product_part(attended_rows[m], d_last[m])) for m in both]

    act_last = [after(act_last[m], *sent) for m in both]
    branch2 = col_end([branch2_make(m, act_last[m]) for m in both], branch2_col, *sent)
    results = [middle[m] + mod[m, 5] * branch2[m] for m in both]
    d_gate2 = [jnp.sum(cotangents[m] * branch2[m], axis=0) for m in both]
    proj_y = y_start(
        [product_part(attended_rows[m], d_last[m]) for m in both], [s[1] for s in proj_core]
    )

    d_projected, qkv_core, qkv_y = [], [], []
    later = [proj_y[0], fc2_z[0], *d_gate2]

    def qkv_part(g, m):
        joined = jnp.concatenate(d_projected[g][m], axis=1)
        return product_part(hidden1_rows[m], joined)

    for g in range(groups):
        makes = [attended_make(m, g, d_branch1[m]) for m in both]
        d_attended = [d.astype(bf16) for d in col_end(makes, attended_col[g], *later)]
        d_attended[1] = padded(d_attended[1])
        if kernels:
            outs = attend_back(
                projected[0], projected[1], real, g * pairs, pairs, *d_attended, lse[g]
            )
        else:
            outs = plain_attend_back(projected[0], projected[1], real, *d_attended, lse[g])
        d_projected.append([[outs[2 * j + m] for j in range(3)] for m in both])
        if g + 1 < groups:
            qkv_core.append([core_start(qkv_part(g, m)) for m in both])
            later = [qkv_core[g][m][0] for m in both]
            if g > 0:
                gots = [after(s[1], *later) for s in qkv_core[g - 1]]
                qkv_y.append(y_start([qkv_part(g - 1, m) for m in both], gots))
                later.append(qkv_y[g - 1][0])
            if g + 2 == groups:
                fc1_z = z_start([fc1_y], fc2_z, *later)
                later.append(fc1_z[0])

    d_all = [
        jnp.concatenate(
            [d_projected[g][m][j] for j in range(3) for g in range(groups)], axis=1
        )[: counts[m]]
        for m in both
    ]

    def hidden1_make(m, d):
        return lambda c: dot(
            "te,de->td", d, lax.dynamic_slice(first_full, (m, c * w, 0), (1, w, 3 * w))[0]
        )

    hidden1_col = col_start([hidden1_make(m, d_all[m]) for m in both])
    if groups == 1:
        fc1_z = z_start([fc1_y], fc2_z)
    g = groups - 1
    d_projected[g] = [
        [after(d_projected[g][m][0], hidden1_col[0]), *d_projected[g][m][1:]] for m in both
    ]
    qkv_core.append([core_start(qkv_part(g, m)) for m in both])
    for g in range(len(qkv_y), groups):
        qkv_y.append(y_start([qkv_part(g, m) for m in both], [s[1] for s in qkv_core[g]]))
    first_z = z_start([proj_y, *qkv_y[: groups // 2]], fc1_z, hidden1_col[0])

    d_gate1 = [jnp.sum(d_middle[m] * branch1[m], axis=0) for m in both]
    d_shift2 = [jnp.sum(d_hidden2[m], axis=0) for m in both]
    d_scale2 = [jnp.sum(d_hidden2[m] * norm2[m], axis=0) for m in both]

    d_hidden1 = col_end([hidden1_make(m, d_all[m]) for m in both], hidden1_col)
    d_hidden1 = [d.astype(bf16) for d in d_hidden1]
    last_z = z_start(qkv_y[groups // 2 :], first_z, *d_hidden1)
    d_hidden1 = [d.astype(f32) for d in d_hidden1]
    d_shift1 = [jnp.sum(d_hidden1[m], axis=0) for m in both]
    d_scale1 = [jnp.sum(d_hidden1[m] * norm1[m], axis=0) for m in both]
    back1 = norm_back(d_hidden1, norm1, rstd1, [mod[m, 1] for m in both])
    grad_inputs = [d_middle[m] + back1[m] for m in both]

    d_mod = jnp.concatenate(
        [
            part[m].reshape(1, w)
            for m in both
            for part in (d_shift1, d_scale1, d_gate1, d_shift2, d_scale2, d_gate2)
        ],
        axis=1,
    ).astype(bf16)
    d_mod_all = lax.all_to_all(jnp.broadcast_to(d_mod, (R, 12 * w)), "row", 0, 0, tiled=True)
    grad_ada = dot("sd,se->de", silu_rows, d_mod_all)
    d_silu = dot("se,de->sd", d_mod_all, ada_shard)
    d_silu = jnp.broadcast_to(d_silu[:, None], (R, C, fan)).reshape(R * C, fan)
    d_silu = lax.all_to_all(d_silu, ("row", "col"), 0, 0, tiled=True).reshape(C, R // C, C, fan)
    d_silu = lax.dynamic_index_in_dim(d_silu, me_c, 0, keepdims=False)
    d_silu = jnp.sum(d_silu, axis=1).reshape(1, w)
    _, pullback = jax.vjp(jax.nn.silu, conditioning)
    grad_cond = pullback(d_silu)[0]

    grad_fc2 = unmove_units(fc2_z[1].astype(f32))
    grad_fc1 = unmove_columns(fc1_z[1].astype(f32)).reshape(fan, 2, units)
    grad_proj = first_z[1][:, : 2 * w].astype(f32)
    grad_qkv = jnp.concatenate([first_z[1][:, 2 * w :], last_z[1]], axis=1).astype(f32)
    grad_qkv = jnp.concatenate(
        [
            grad_qkv[:, ((2 * g + m) * 3 + j) * wide : ((2 * g + m) * 3 + j + 1) * wide]
            for m in both
            for j in range(3)
            for g in range(groups)
        ],
        axis=1,
    )

    def stored(gradient):
        return gradient.reshape(gradient.shape[0], 1, -1)

    return (
        pack(results[0]).astype(bf16),
        pack(results[1]).astype(bf16),
        pack(grad_inputs[0]),
        pack(grad_inputs[1]),
        grad_cond,
        stored(grad_ada),
        stored(grad_qkv),
        stored(grad_proj),
        grad_fc1,
        stored(grad_fc2),
    )


def solution(mesh):
    tokens = P("row", "col", None)
    units = P("row", None, "col")
    cond = P("row", "col")
    return jax.shard_map(
        partial(per_device, mesh.shape["row"], mesh.shape["col"]),
        mesh=mesh,
        in_specs=(tokens, tokens, cond, tokens, tokens, tokens, units, tokens, tokens, tokens),
        out_specs=(tokens, tokens, tokens, tokens, cond, tokens, tokens, tokens, units, tokens),
        check_vma=False,
    )
```

```python
from functools import partial

import jax
import jax.numpy as jnp
from jax import lax
from jax.experimental import pallas as pl
from jax.experimental.pallas import tpu as pltpu
from jax.sharding import PartitionSpec as P

MODEL_WIDTH = 1536
HEAD_DIM = 64
FEEDFORWARD_UNITS = 6144
EPSILON = 1e-06
PAIR = 2 * HEAD_DIM
BLOCK = 256
MASKED = -1e30

bf16 = jnp.bfloat16
f32 = jnp.float32


def dot(spec, a, b):
    return jnp.einsum(spec, a, b, preferred_element_type=f32)


def mm_nn(a, b):
    return lax.dot_general(a, b, (((1,), (0,)), ((), ())), preferred_element_type=f32)


def mm_nt(a, b):
    return lax.dot_general(a, b, (((1,), (1,)), ((), ())), preferred_element_type=f32)


def attend_kernel(real, qi, qt, ki, kt, vi, vt, oi, ot, lse, q_s, k_s, v_s, s_0, s_1):
    ni, n, nk = qi.shape[0], q_s.shape[0], k_s.shape[0]
    scale = jnp.asarray(HEAD_DIM**-0.5, bf16)
    q_s[:ni, :] = qi[...] * scale
    q_s[ni:, :] = qt[...] * scale
    k_s[:ni, :] = ki[...]
    k_s[ni:, :] = kt[: nk - ni, :]
    v_s[:, :ni] = vi[...].T
    v_s[:, ni:] = vt[...].T[:, : nk - ni]
    key = lax.broadcasted_iota(jnp.int32, (nk - ni, BLOCK), 0)
    held = (s_0, s_1)

    def scores(i, h):
        head = slice(h * HEAD_DIM, (h + 1) * HEAD_DIM)
        held[h][...] = mm_nt(k_s[:, head], q_s[i * BLOCK : (i + 1) * BLOCK, head])

    def mix(i, h):
        head = slice(h * HEAD_DIM, (h + 1) * HEAD_DIM)
        s = held[h][...]
        s_i, s_t = s[:ni], jnp.where(key < real, s[ni:], MASKED)
        top = jnp.maximum(
            jnp.max(s_i, axis=0, keepdims=True), jnp.max(s_t, axis=0, keepdims=True)
        )
        e_i, e_t = jnp.exp(s_i - top), jnp.exp(s_t - top)
        total = jnp.sum(e_i, axis=0, keepdims=True) + jnp.sum(e_t, axis=0, keepdims=True)
        part = 1.0 / total
        lse[0, h : h + 1, i * BLOCK : (i + 1) * BLOCK] = top + jnp.log(total)
        return mm_nn(v_s[head, :ni], (e_i * part).astype(bf16)) + mm_nn(
            v_s[head, ni:], (e_t * part).astype(bf16)
        )

    blocks = n // BLOCK
    scores(0, 0)
    for i in range(blocks):
        scores(i, 1)
        first = mix(i, 0)
        if i + 1 < blocks:
            scores(i + 1, 0)
        out = jnp.concatenate([first, mix(i, 1)], axis=0).T.astype(bf16)
        if i * BLOCK < ni:
            oi[i * BLOCK : (i + 1) * BLOCK, :] = out
        else:
            ot[i * BLOCK - ni : (i + 1) * BLOCK - ni, :] = out


def attend_back_kernel(
    real, pairs, qi, qt, ki, kt, vi, vt, di, dt, lse, *rest
):
    out_i, out_t, q_s, k_s, kt_s, v_s, d_s, dq_s, dk_s, dv_s = rest[-10:]
    ni, n, nk = qi.shape[0], q_s.shape[0], k_s.shape[0]
    nt = nk - ni
    scale = HEAD_DIM**-0.5
    q_s[:ni, :] = qi[...] * jnp.asarray(scale, bf16)
    q_s[ni:, :] = qt[...] * jnp.asarray(scale, bf16)
    k_s[:ni, :] = ki[...]
    k_s[ni:, :] = kt[:nt, :]
    kt_s[:, :ni] = ki[...].T
    kt_s[:, ni:] = kt[...].T[:, :nt]
    v_s[:ni, :] = vi[...]
    v_s[ni:, :] = vt[:nt, :]
    d_s[:ni, :] = di[...]
    d_s[ni:, :] = dt[...]
    key = lax.broadcasted_iota(jnp.int32, (nt, BLOCK), 0)
    for i in range(n // BLOCK):
        rows = slice(i * BLOCK, (i + 1) * BLOCK)
        dq = []
        for h in range(2):
            head = slice(h * HEAD_DIM, (h + 1) * HEAD_DIM)
            q, d = q_s[rows, head], d_s[rows, head]
            s = mm_nt(k_s[:, head], q)
            s = jnp.concatenate([s[:ni], jnp.where(key < real, s[ni:], MASKED)], axis=0)
            p = jnp.exp(s - lse[0, h : h + 1, rows])
            t = p * mm_nt(v_s[:, head], d)
            d_scores = (t - p * jnp.sum(t, axis=0, keepdims=True)).astype(bf16)
            dv, dk = mm_nn(p.astype(bf16), d), mm_nn(d_scores, q)
            if i == 0:
                dv_s[:, head] = dv
                dk_s[:, head] = dk
            else:
                dv_s[:, head] += dv
                dk_s[:, head] += dk
            dq.append(mm_nn(kt_s[head, :], d_scores))
        dq_s[:, rows] = jnp.concatenate(dq, axis=0)
    d_q = (dq_s[...] * scale).T.astype(bf16)
    at = pl.program_id(0)

    def lanes(j):
        return pl.ds(pl.multiple_of((j * pairs + at) * PAIR, PAIR), PAIR)

    out_i[:, lanes(0)] = d_q[:ni]
    out_t[:, lanes(0)] = d_q[ni:]
    for j, total in ((1, dk_s), (2, dv_s)):
        out_i[:, lanes(j)] = total[:ni, :].astype(bf16)
        out_t[:nt, lanes(j)] = total[ni:, :].astype(bf16)
        out_t[nt:, lanes(j)] = jnp.zeros((n - nk, PAIR), bf16)


def projection_specs(ni, nt, group, pairs):
    specs = []
    for j in range(3):
        at = lambda p, j=j: (0, (3 * group + j) * pairs + p)
        specs += [pl.BlockSpec((ni, PAIR), at), pl.BlockSpec((nt, PAIR), at)]
    return specs


def attend(image, text, real, group, pairs):
    ni, nt = image.shape[0], text.shape[0]
    n = ni + nt
    nk = ni + (real + 15) // 16 * 16
    at = lambda p: (0, p)
    return pl.pallas_call(
        partial(attend_kernel, real),
        grid=(pairs,),
        in_specs=projection_specs(ni, nt, group, pairs),
        out_specs=[
            pl.BlockSpec((ni, PAIR), at),
            pl.BlockSpec((nt, PAIR), at),
            pl.BlockSpec((1, 2, n), lambda p: (p, 0, 0)),
        ],
        out_shape=[
            jax.ShapeDtypeStruct((ni, pairs * PAIR), bf16),
            jax.ShapeDtypeStruct((nt, pairs * PAIR), bf16),
            jax.ShapeDtypeStruct((pairs, 2, n), f32),
        ],
        scratch_shapes=[
            pltpu.VMEM((n, PAIR), bf16),
            pltpu.VMEM((nk, PAIR), bf16),
            pltpu.VMEM((PAIR, nk), bf16),
            pltpu.VMEM((nk, BLOCK), f32),
            pltpu.VMEM((nk, BLOCK), f32),
        ],
        compiler_params=pltpu.CompilerParams(vmem_limit_bytes=40 * 2**20),
        cost_estimate=pl.CostEstimate(
            flops=pairs * 2 * n * n * 256 * 2 * 2,
            bytes_accessed=pairs * n * PAIR * 2 * 4,
            transcendentals=pairs * 2 * n * n,
        ),
    )(image, text, image, text, image, text)


def attend_back(image, text, real, group, pairs, d_image, d_text, lse, filled):
    ni, nt = image.shape[0], text.shape[0]
    n = ni + nt
    nk = ni + (real + 15) // 16 * 16
    at = lambda p: (0, p)
    one_i, one_t = pl.BlockSpec((ni, PAIR), at), pl.BlockSpec((nt, PAIR), at)
    wide = 3 * pairs * PAIR
    return pl.pallas_call(
        partial(attend_back_kernel, real, pairs),
        grid=(pairs,),
        in_specs=projection_specs(ni, nt, group, pairs)
        + [one_i, one_t, pl.BlockSpec((1, 2, n), lambda p: (p, 0, 0))]
        + [pl.BlockSpec(memory_space=pl.ANY)] * len(filled),
        out_specs=[pl.BlockSpec((n_, wide), lambda p: (0, group)) for n_ in (ni, nt)],
        out_shape=[jax.ShapeDtypeStruct(a.shape, bf16) for a in (image, text)],
        input_output_aliases={9: 0, 10: 1} if filled else {},
        scratch_shapes=[
            pltpu.VMEM((n, PAIR), bf16),
            pltpu.VMEM((nk, PAIR), bf16),
            pltpu.VMEM((PAIR, nk), bf16),
            pltpu.VMEM((nk, PAIR), bf16),
            pltpu.VMEM((n, PAIR), bf16),
            pltpu.VMEM((PAIR, n), f32),
            pltpu.VMEM((nk, PAIR), f32),
            pltpu.VMEM((nk, PAIR), f32),
        ],
        compiler_params=pltpu.CompilerParams(vmem_limit_bytes=40 * 2**20),
        cost_estimate=pl.CostEstimate(
            flops=pairs * 2 * n * n * 256 * 2 * 5,
            bytes_accessed=pairs * n * PAIR * 2 * 8,
            transcendentals=pairs * 2 * n * n,
        ),
    )(image, text, image, text, image, text, d_image, d_text, lse, *filled)


def split_heads(a):
    return a.reshape(a.shape[0], -1, HEAD_DIM)


def plain_attend(image, text, real):
    joined = jnp.concatenate([image, text[:real]], axis=0)
    q, k, v = (split_heads(a) for a in jnp.split(joined, 3, axis=1))
    scores = dot("qhd,khd->hqk", q, k) * HEAD_DIM ** (-0.5)
    top = jnp.max(scores, axis=-1, keepdims=True)
    expo = jnp.exp(scores - top)
    total = jnp.sum(expo, axis=-1, keepdims=True)
    out = dot("hqk,khd->qhd", (expo / total).astype(bf16), v).astype(bf16)
    out = out.reshape(joined.shape[0], -1)
    pad = ((0, text.shape[0] - real), (0, 0))
    ni = image.shape[0]
    return out[:ni], jnp.pad(out[ni:], pad), top + jnp.log(total)


def plain_attend_back(image, text, real, d_image, d_text, lse):
    ni, width = image.shape[0], d_image.shape[1]
    joined = jnp.concatenate([image, text[:real]], axis=0)
    q, k, v = (split_heads(a) for a in jnp.split(joined, 3, axis=1))
    d = split_heads(jnp.concatenate([d_image, d_text[:real]], axis=0))
    factor = HEAD_DIM ** (-0.5)
    probs = jnp.exp(dot("qhd,khd->hqk", q, k) * factor - lse)
    d_v = dot("hqk,qhd->khd", probs.astype(bf16), d)
    d_probs = dot("qhd,khd->hqk", d, v)
    d_scores = probs * (d_probs - jnp.sum(d_probs * probs, axis=-1, keepdims=True))
    d_scores = d_scores.astype(bf16)
    d_q = dot("hqk,khd->qhd", d_scores, k) * factor
    d_k = dot("hqk,qhd->khd", d_scores, q) * factor
    out = jnp.concatenate([g.reshape(-1, width).astype(bf16) for g in (d_q, d_k, d_v)], axis=1)
    return out[:ni], jnp.pad(out[ni:], ((0, text.shape[0] - real), (0, 0)))


def gelu_both(v):
    root = (2.0 / jnp.pi) ** 0.5
    t = jnp.tanh(root * (v + 0.044715 * (v * v * v)))
    half = 0.5 * (1.0 + t)
    slope = half + 0.5 * v * (1.0 - t * t) * (root * (1.0 + 3.0 * 0.044715 * (v * v)))
    return v * half, slope


def row_factors(rows):
    if rows % 4 == 0:
        z = 4 if rows >= 16 else 2
        return z, rows // 2 // z
    return 1, rows // 2


def after(value, *earlier):
    return lax.optimization_barrier((value, *earlier))[0]


def per_device(
    R,
    C,
    image_tokens,
    text_tokens,
    conditioning,
    ada_weight,
    qkv_weight,
    proj_weight,
    fc1_weight,
    fc2_weight,
    image_cotangent,
    text_cotangent,
):
    w = image_tokens.shape[2] // 2
    me_r = lax.axis_index("row")
    me_c = lax.axis_index("col")
    Z, Y = row_factors(R)
    ZY = Z * Y
    my_core = me_r % 2
    my_y = (me_r // 2) % Y
    pair = C == 2
    parity = pair and (R // C) % C == 0
    kernels = w % PAIR == 0
    both = range(2)
    CORE = [(r, r ^ 1) for r in range(R)]
    YSWAP = [(r, r ^ 2) for r in range(R)]
    YGROUPS = [[(z * Y + y) * 2 + c for y in range(Y)] for z in range(Z) for c in range(2)]
    ZGROUPS = [[(z * Y + y) * 2 + c for z in range(Z)] for y in range(Y) for c in range(2)]
    ZYGROUPS = [[2 * k + c for k in range(ZY)] for c in range(2)]
    XSWAP = [(0, 1), (1, 0)]

    def swap(a):
        return lax.ppermute(a, "col", XSWAP)

    def natural(own, other, axis=-1):
        first = jnp.where(me_c == 0, own, other)
        second = jnp.where(me_c == 0, other, own)
        return jnp.concatenate([first, second], axis=axis)

    def send(own):
        if pair:
            return swap(own)
        return lax.all_gather(own, "col", axis=own.ndim - 1, tiled=True)

    def whole(own, got):
        return natural(own, got) if pair else got

    def gather_features(own):
        return whole(own, send(own))

    def col_start(makes, wait=False):
        if pair:
            sent = jnp.concatenate([make(1 - me_c).astype(bf16) for make in makes], axis=0)
            return sent, None if wait else swap(sent)
        sent = jnp.concatenate(
            [jnp.concatenate([make(c) for c in range(C)], axis=-1) for make in makes], axis=0
        )
        return sent, lax.psum_scatter(sent, "col", scatter_dimension=1, tiled=True)

    def col_end(makes, state, *earlier):
        got = after(state[1], *earlier)
        parts = (got[: counts[0]].astype(f32), got[counts[0] :].astype(f32))
        return [make(me_c) + part if pair else part for make, part in zip(makes, parts)]

    def sum_col(a):
        return lax.psum(a, "col")

    def core_start(part):
        sent = part[0]().astype(bf16)
        return sent, lax.ppermute(sent, "row", CORE)

    def y_start(parts, gots):
        owns = [
            [share() + take(got).astype(f32) for share, take in part[1]]
            for part, got in zip(parts, gots)
        ]
        if Y == 2:
            owns = [[own.reshape(Z, own.shape[0] // Z, -1) for own in pieces] for pieces in owns]
            sent = jnp.concatenate([pieces[0].astype(bf16) for pieces in owns], axis=2)
            return sent, [pieces[1] for pieces in owns], lax.ppermute(sent, "row", YSWAP)
        own = jnp.concatenate([pieces[0] for pieces in owns], axis=1)
        own = own.reshape(Z, Y, own.shape[0] // ZY, -1).astype(bf16)
        if Y > 1:
            own = lax.psum_scatter(own, "row", scatter_dimension=1, axis_index_groups=YGROUPS)
        else:
            own = own[:, 0]
        return own, [own], None

    def z_start(states, previous, *earlier):
        pieces = []
        for _, kept, got in states:
            if got is not None:
                got, at, own, kept = after(got, *earlier), 0, kept, []
                for a in own:
                    kept.append((a + got[:, :, at : at + a.shape[2]].astype(f32)).astype(bf16))
                    at += a.shape[2]
            pieces += kept
        kept = jnp.concatenate(pieces, axis=2)
        if Z == 1:
            return [kept, kept[0]]
        if previous is not None:
            kept, previous[1] = lax.optimization_barrier((kept, previous[1]))
        summed = lax.psum_scatter(kept, "row", scatter_dimension=0, axis_index_groups=ZGROUPS)
        return [kept, summed]

    def both_start(parts, gots):
        own = [share() + got.astype(f32) for share, got in zip(parts, gots)]
        own = jnp.concatenate([a.astype(bf16) for a in own], axis=1)
        own = own.reshape(ZY, own.shape[0] // ZY, -1)
        return [
            own,
            lax.psum_scatter(own, "row", scatter_dimension=0, axis_index_groups=ZYGROUPS),
        ]

    def rows_of(a, small=False, plain=Y != 2):
        t, width = a.shape
        blk = width // R
        if plain and not small:
            parts = a.reshape(t, ZY, 2, blk)
            other, own = (
                lax.dynamic_index_in_dim(parts, core, 2, keepdims=False).reshape(t, width // 2)
                for core in (1 - my_core, my_core)
            )
            return other, [own]
        if small:
            at = jnp.arange(width)
            core, y = at // (width // 2), at // (width // 4) % 2
            core = jnp.where(core == 0, 1 - my_core, my_core)
            y = jnp.where(y == 0, 1 - my_y, my_y)
            row = (at // blk % ZY if plain else at // blk % Z * Y + y) * 2 + core
            pick = (row * blk + at % blk)[None, :] == jnp.arange(width)[:, None]
            picked = dot("tp,pq->tq", a, pick.astype(bf16)).astype(bf16)
            half, quarter = width // 2, width // 4
            if plain:
                return picked[:, :half], [picked[:, half:]]
            return picked[:, :half], [picked[:, half : half + quarter], picked[:, -quarter:]]
        parts = a.reshape(t, Z, Y, 2, blk)

        def pick_rows(core, y):
            got = lax.dynamic_index_in_dim(parts, core, 3, keepdims=False)
            return lax.dynamic_index_in_dim(got, y, 2, keepdims=False).reshape(t, Z * blk)

        other = jnp.concatenate(
            [pick_rows(1 - my_core, 1 - my_y), pick_rows(1 - my_core, my_y)], axis=1
        )
        return other, [pick_rows(my_core, 1 - my_y), pick_rows(my_core, my_y)]

    def rows_of_both(pair_of, **how):
        return [rows_of(pair_of[0], **how), rows_of(pair_of[1], small=True, **how)]

    def product_part(rows, b):
        other, own = rows
        size = other.shape[1] // len(own)

        def share(a):
            return lambda: dot("tp,tn->pn", a, b)

        def take(i):
            return lambda got: got[i * size : (i + 1) * size]

        return share(other), [(share(a), take(i)) for i, a in enumerate(own)]

    def unpack(packed):
        rows = packed.reshape(packed.shape[0], 2 * w)
        return jnp.concatenate([rows[:, :w], rows[:, w:]], axis=0)

    def pack(plain):
        half = plain.shape[0] // 2
        return jnp.concatenate([plain[:half], plain[half:]], axis=1).reshape(half, 1, 2 * w)

    def gather_rows(a, order=None):
        return lax.all_gather(a, "row", axis=1, tiled=True, axis_index_groups=order)

    total = w // PAIR
    groups = (3 if total % 3 == 0 else 1) if kernels else 1
    pairs = total // groups
    wide = w // groups
    fan = MODEL_WIDTH // R
    qkv_shard = qkv_weight.reshape(fan, 6 * w)
    proj_shard = proj_weight.reshape(fan, 2 * w)
    first_shard = jnp.stack(
        [
            jnp.concatenate(
                [
                    qkv_shard[:, (3 * m + j) * w + g * wide :][:, :wide].astype(bf16)
                    for g in range(groups)
                    for j in range(3)
                ]
                + [
                    proj_shard[:, m * w : (m + 1) * w].astype(bf16),
                ],
                axis=1,
            )
            for m in both
        ]
    )
    first_full = gather_rows(first_shard)
    qkv_full = [first_full[m, :, : 3 * w] for m in both]
    proj_full = [first_full[m, :, 3 * w :] for m in both]

    silu_own = jax.nn.silu(conditioning).astype(bf16).reshape(R // C, 1, fan)
    silu_sent = jnp.broadcast_to(silu_own[None], (C, R // C, C, fan)).reshape(R * C, fan)
    silu_got = lax.all_to_all(silu_sent, ("row", "col"), 0, 0, tiled=True).reshape(R, C, fan)
    silu_rows = lax.dynamic_index_in_dim(silu_got, me_r // (R // C), 1, keepdims=False)
    ada_shard = ada_weight.reshape(fan, 12 * w).astype(bf16)
    mod = lax.all_to_all(dot("sd,de->se", silu_rows, ada_shard), "row", 0, 0, tiled=True)
    mod = jnp.sum(mod, axis=0).reshape(2, 6, w)

    packed = (image_tokens, text_tokens)
    packed_got = None
    if pair:
        packed_got = swap(jnp.concatenate(packed, axis=0))
        packed_got = [packed_got[: packed[0].shape[0]], packed_got[packed[0].shape[0] :]]
    first_mod = gather_features(mod[:, 0:2].reshape(4, w)).reshape(2, 2, MODEL_WIDTH)
    inputs = [unpack(p).astype(f32) for p in packed]
    cotangents = [unpack(p).astype(f32) for p in (image_cotangent, text_cotangent)]
    counts = [a.shape[0] for a in inputs]
    real = counts[1]
    padding = -(counts[0] + real) % BLOCK
    d_branch2 = [(mod[m, 5] * cotangents[m]).astype(bf16) for m in both]

    fc1_weight, fc2_weight = lax.optimization_barrier((fc1_weight, fc2_weight, silu_got))[:2]
    fc1_shard = jnp.stack([fc1_weight[:, m] for m in both]).astype(bf16)
    blk2 = fc2_weight.shape[0]
    fc2_shard = fc2_weight.reshape(blk2, 2 * w)
    fc2_shard = jnp.stack([fc2_shard[:, m * w : (m + 1) * w] for m in both]).astype(bf16)
    units = fc1_shard.shape[2]
    blocks = units // blk2

    if parity:
        half = blocks // 2
        MOVES = [(r * C + c, ((r // C) * C + c) * C + r % C) for r in range(R) for c in range(C)]
        MOVES = [(a, b) for a, b in MOVES if a != b]
        stays = me_r % C == me_c
        ORDER = [[k * C + c for c in range(C) for k in range(R // C)]]

        def move_units(a, *earlier):
            moved = lax.ppermute(a, ("row", "col"), MOVES)
            return jnp.where(stays, a, after(moved, *earlier) if earlier else moved)

        unmove_units = move_units
        group = fc1_shard.reshape(2, fan, half, 2, blk2)
        mine = lax.dynamic_index_in_dim(group, me_c, 3, keepdims=False)
        theirs = swap(lax.dynamic_index_in_dim(group, 1 - me_c, 3, keepdims=False))

        def moved_columns(*earlier):
            return natural(mine, after(theirs, *earlier), axis=2).reshape(fc1_shard.shape)

        def unmove_columns(g):
            g = g.reshape(fan, 2, blocks, blk2)
            first, second = g[:, :, :half], g[:, :, half:]
            mine = jnp.where(me_c == 0, first, second)
            theirs = swap(jnp.where(me_c == 0, second, first))
            even = jnp.where(me_c == 0, mine, theirs)
            odd = jnp.where(me_c == 0, theirs, mine)
            return jnp.stack([even, odd], axis=3).reshape(fan, 2, units)

    else:
        MOVES = [
            (r * C + c, (c * (R // C) + r % (R // C)) * C + r // (R // C))
            for r in range(R)
            for c in range(C)
        ]
        ORDER = None

        def move_units(a, *earlier):
            return lax.ppermute(a, ("row", "col"), MOVES)

        def moved_columns(*earlier):
            return fc1_shard

        def unmove_units(a):
            return lax.ppermute(a, ("row", "col"), [(b, a) for a, b in MOVES])

        def unmove_columns(g):
            return g


    def padded(a):
        return jnp.pad(a, ((0, padding), (0, 0)))

    if pair:
        inputs_full = [natural(unpack(packed[m]), unpack(packed_got[m])) for m in both]
    else:
        inputs_full = [gather_features(unpack(p)) for p in packed]

    mean1, rstd1, hidden1 = [], [], []
    for m in both:
        x = inputs_full[m].astype(f32)
        mean = jnp.sum(x, axis=-1, keepdims=True) / MODEL_WIDTH
        meansq = jnp.sum(x * x, axis=-1, keepdims=True) / MODEL_WIDTH
        rstd = lax.rsqrt(meansq - mean * mean + EPSILON)
        mean1.append(mean)
        rstd1.append(rstd)
        hidden1.append(
            ((x - mean) * rstd * (1.0 + first_mod[m, 1]) + first_mod[m, 0]).astype(bf16)
        )
    hidden1[1] = padded(hidden1[1])
    norm1 = [(inputs[m] - mean1[m]) * rstd1[m] for m in both]
    fc1_moved = moved_columns(*hidden1)
    fc1_full = gather_rows(fc1_moved)
    d_branch2_own = jnp.concatenate(d_branch2, axis=0)
    d_branch2_got = send(d_branch2_own)
    fc2_shard = after(fc2_shard, d_branch2_got)
    hidden1_in = [after(hidden1[0], d_branch2_got), hidden1[1]]
    projected = [dot("td,de->te", hidden1_in[m], qkv_full[m]).astype(bf16) for m in both]
    fc2_moved = move_units(fc2_shard, *projected)
    fc2_full = gather_rows(fc2_moved, ORDER).reshape(2, C, units, w)

    attended, attended_got, lse = [], [], []
    for g in range(groups):
        text = projected[1]
        if g > 1:
            text = after(text, attended_got[g - 2])
        if kernels:
            out_i, out_t, saved = attend(projected[0], text, real, g, pairs)
        else:
            out_i, out_t, saved = plain_attend(projected[0], text, real)
        attended.append(jnp.concatenate([out_i, out_t[:real]], axis=0))
        attended_got.append(send(attended[g]))
        lse.append(saved)
    attended_full = whole(
        jnp.concatenate(attended, axis=1), jnp.concatenate(attended_got, axis=1)
    )
    attended_full = [attended_full[: counts[0]], attended_full[counts[0] :]]
    attended_rows, hidden1_rows = rows_of_both(attended_full), rows_of_both(hidden1)

    branch1 = [dot("te,eb->tb", attended_full[m], proj_full[m]) for m in both]
    middle = [inputs[m] + mod[m, 2] * branch1[m] for m in both]

    def token_sums(firsts, seconds):
        own = jnp.concatenate(
            [
                jnp.stack([jnp.sum(firsts[m], axis=-1), jnp.sum(seconds[m], axis=-1)])
                for m in both
            ],
            axis=1,
        )
        sums = sum_col(own) / MODEL_WIDTH
        parts = (sums[:, : counts[0]], sums[:, counts[0] :])
        return [(p[0][:, None], p[1][:, None]) for p in parts]

    stats = token_sums(middle, [a * a for a in middle])
    rstd2 = [lax.rsqrt(sq - mean * mean + EPSILON) for mean, sq in stats]
    norm2 = [(middle[m] - stats[m][0]) * rstd2[m] for m in both]
    hidden2 = [(norm2[m] * (1.0 + mod[m, 4]) + mod[m, 3]).astype(bf16) for m in both]
    hidden2[0] = after(hidden2[0], hidden2[1])
    hidden2_got = [send(a) for a in hidden2]
    hidden2_got[0], attended_rows, hidden1_rows = lax.optimization_barrier(
        (hidden2_got[0], attended_rows, hidden1_rows)
    )
    hidden2_full = [whole(a, got) for a, got in zip(hidden2, hidden2_got)]
    d_branch2_full = whole(d_branch2_own, after(d_branch2_got, hidden2[0]))
    d_branch2_full = [d_branch2_full[: counts[0]], d_branch2_full[counts[0] :]]
    hidden2_rows = rows_of_both(hidden2_full, plain=True)
    preact = [dot("td,df->tf", hidden2_full[m], fc1_full[m]) for m in both]
    pairs_of = [gelu_both(a) for a in preact]
    activated = [a.astype(bf16) for a, _ in pairs_of]
    slope = [s for _, s in pairs_of]

    def fc2_part(m, act):
        def share(a, core):
            grad = d_branch2_full[m]
            if parity:
                grad = lax.dynamic_slice_in_dim(grad, core * w, w, 1)
                return lambda: dot("tf,te->fe", a, grad)
            shares = [dot("tf,te->fe", a, grad[:, c * w : (c + 1) * w]) for c in range(C)]
            shares = jnp.concatenate(shares, axis=0).reshape(ZY, 2, blk2, w)
            one = lax.dynamic_index_in_dim(shares, core, 1, keepdims=False)
            return lambda: one.reshape(ZY * blk2, w)

        return share(act, 1 - my_core), share(act, my_core)

    fc2_core = [core_start(fc2_part(m, activated[m])) for m in both]
    act_later = [after(activated[m], *[s[0] for s in fc2_core]) for m in both]
    fc2_z = both_start(
        [fc2_part(m, act_later[m])[1] for m in both], [s[1] for s in fc2_core]
    )
    grads = [after(d_branch2_full[m], fc2_z[0]) for m in both]
    none = jnp.minimum(me_r, 0)
    d_activated = [
        dot(
            "tce,cfe->tf",
            grads[m].reshape(-1, C, w),
            lax.dynamic_slice(fc2_full, (m + none, 0, 0, 0), (1, C, units, w))[0],
        )
        for m in both
    ]
    d_preact = [(d_activated[m] * slope[m]).astype(bf16) for m in both]

    def hidden2_make(m, d):
        return lambda c: dot(
            "tf,df->td", d, lax.dynamic_slice(fc1_full, (m, c * w, 0), (1, w, units))[0]
        )

    hidden2_col = col_start([hidden2_make(m, d_preact[m]) for m in both])

    d_next = [after(d_preact[m], hidden2_col[0]) for m in both]
    fc1_core = [core_start(product_part(hidden2_rows[m], d_next[m])) for m in both]
    fc1_sent = [s[0] for s in fc1_core]

    def branch2_make(m, act):
        return lambda c: dot(
            "tf,fe->te", act, lax.dynamic_slice(fc2_full, (m, c, 0, 0), (1, 1, units, w))[0, 0]
        )

    act_last = [after(activated[m], *fc1_sent) for m in both]
    branch2_col = col_start([branch2_make(m, act_last[m]) for m in both], wait=True)
    d_next = [after(d_next[m], branch2_col[0]) for m in both]
    fc1_z = both_start(
        [product_part(hidden2_rows[m], d_next[m])[1][0][0] for m in both],
        [s[1] for s in fc1_core],
    )
    d_hidden2 = col_end(
        [hidden2_make(m, d_next[m]) for m in both], hidden2_col, branch2_col[0], fc1_z[0]
    )
    d_hidden2 = [d.astype(bf16).astype(f32) for d in d_hidden2]

    def norm_back(d_hidden, norm, rstd, scale, between=None):
        d_norm = [d_hidden[m] * (1.0 + scale[m]) for m in both]
        sums = token_sums(d_norm, [d_norm[m] * norm[m] for m in both])
        if between is not None:
            sums = between(sums)
        return [rstd[m] * (d_norm[m] - sums[m][0] - norm[m] * sums[m][1]) for m in both]

    back2 = norm_back(d_hidden2, norm2, rstd2, [mod[m, 4] for m in both])
    d_middle = [cotangents[m] + back2[m] for m in both]
    d_branch1 = [(mod[m, 2] * d_middle[m]).astype(bf16) for m in both]

    def attended_make(m, g, d):
        return lambda c: dot(
            "tv,yv->ty",
            d,
            lax.dynamic_slice(first_full, (m, c * w + g * wide, 3 * w), (1, wide, w))[0],
        )

    attended_col = [col_start([attended_make(m, 0, d_branch1[m]) for m in both])]
    d_last = [after(d_branch1[m], attended_col[0][0]) for m in both]
    proj_core = [core_start(product_part(attended_rows[m], d_last[m])) for m in both]

    d_projected, qkv_core, qkv_y = [], [], []
    later = [s[0] for s in proj_core]

    def qkv_part(g, m):
        return product_part(hidden1_rows[m], d_projected[m][:, 3 * wide * g :][:, : 3 * wide])

    def hidden1_make(m, d):
        return lambda c: dot(
            "te,de->td", d, lax.dynamic_slice(first_full, (m, c * w, 0), (1, w, 3 * w))[0]
        )

    for g in range(groups):
        makes = [attended_make(m, g, d_branch1[m]) for m in both]
        d_attended = [d.astype(bf16) for d in col_end(makes, attended_col[g], *d_projected)]
        if g + 1 < groups:
            d_following = [after(d_branch1[m], *d_attended) for m in both]
            attended_col.append(
                col_start([attended_make(m, g + 1, d_following[m]) for m in both])
            )
            later = [*later, attended_col[g + 1][0]]
        if pair and g == max(groups - 2, 0):
            branch2_col = branch2_col[0], swap(after(branch2_col[0], attended_col[-1][0]))
        d_attended[1] = after(padded(d_attended[1]), *later)
        if g == 1:
            d_attended[1], fc2_z[1] = lax.optimization_barrier((d_attended[1], fc2_z[1]))
        if kernels:
            filled = d_projected
            if g:
                filled = [after(a, *later) for a in d_projected]
            outs = attend_back(
                projected[0], projected[1], real, g, pairs, *d_attended, lse[g], filled
            )
        else:
            outs = plain_attend_back(projected[0], projected[1], real, *d_attended, lse[g])
        d_projected = list(outs)
        done = list(d_projected)
        later = []
        if g + 1 < groups:
            qkv_core.append([core_start(qkv_part(g, m)) for m in both])
            later += [qkv_core[g][m][0] for m in both]
        if g == 1:
            gots = [after(s[1], *done) for s in proj_core + qkv_core[0]]
            parts = [product_part(attended_rows[m], d_last[m]) for m in both]
            proj_y = y_start(parts + [qkv_part(0, m) for m in both], gots)
            qkv_y.append(None)
            later.append(proj_y[0])
    if groups == 1:
        proj_y = y_start(
            [product_part(attended_rows[m], d_last[m]) for m in both], [s[1] for s in proj_core]
        )

    got = after(branch2_col[1], *done)
    d_projected[1], got = lax.optimization_barrier((d_projected[1], got))
    branch2_col = branch2_col[0], got
    d_all = [d_projected[m][: counts[m]] for m in both]
    hidden1_makes = [hidden1_make(m, d_all[m]) for m in both]
    hidden1_col = col_start(hidden1_makes)
    g = groups - 1
    d_projected = [after(a, hidden1_col[0]) for a in d_projected]
    qkv_core.append([core_start(qkv_part(g, m)) for m in both])
    for g in range(len(qkv_y), groups):
        qkv_y.append(y_start([qkv_part(g, m) for m in both], [s[1] for s in qkv_core[g]]))
    act_last = [after(act_last[m], hidden1_col[0]) for m in both]
    branch2 = col_end([branch2_make(m, act_last[m]) for m in both], branch2_col)
    results = [middle[m] + mod[m, 5] * branch2[m] for m in both]
    d_gate2 = [jnp.sum(cotangents[m] * branch2[m], axis=0) for m in both]

    d_gate1 = [jnp.sum(d_middle[m] * branch1[m], axis=0) for m in both]
    d_shift2 = [jnp.sum(d_hidden2[m], axis=0) for m in both]
    d_scale2 = [jnp.sum(d_hidden2[m] * norm2[m], axis=0) for m in both]

    d_hidden1 = col_end(hidden1_makes, hidden1_col)
    d_hidden1 = [d.astype(bf16) for d in d_hidden1]
    first_z = z_start([proj_y], None, d_hidden1[1])
    d_hidden1[0], fc2_summed = lax.optimization_barrier((d_hidden1[0], fc2_z[1]))
    d_hidden1 = [d.astype(f32) for d in d_hidden1]
    d_shift1 = [jnp.sum(d_hidden1[m], axis=0) for m in both]
    d_scale1 = [jnp.sum(d_hidden1[m] * norm1[m], axis=0) for m in both]
    d_mod = jnp.concatenate(
        [
            part[m].reshape(1, w)
            for m in both
            for part in (d_shift1, d_scale1, d_gate1, d_shift2, d_scale2, d_gate2)
        ],
        axis=1,
    ).astype(bf16)
    d_mod, fc1_summed = lax.optimization_barrier((d_mod, fc1_z[1]))
    last_z = z_start([state for state in qkv_y if state], None, d_mod)
    d_mod_all = lax.all_to_all(jnp.broadcast_to(d_mod, (R, 12 * w)), "row", 0, 0, tiled=True)
    late = {}

    def conditioning_back(sums):
        sums, got = lax.optimization_barrier((sums, d_mod_all))
        late["grad_ada"] = dot("sd,se->de", silu_rows, got)
        d_silu = dot("se,de->sd", got, ada_shard)
        late["fc2"] = unmove_units(fc2_summed.astype(f32))
        late["fc1"] = unmove_columns(fc1_summed.astype(f32)).reshape(fan, 2, units)
        sums, d_silu = lax.optimization_barrier((sums, d_silu))
        d_silu = jnp.broadcast_to(d_silu[:, None], (R, C, fan)).reshape(R * C, fan)
        d_silu = lax.all_to_all(d_silu, ("row", "col"), 0, 0, tiled=True)
        d_silu = d_silu.reshape(C, R // C, C, fan)
        d_silu = lax.dynamic_index_in_dim(d_silu, me_c, 0, keepdims=False)
        late["d_silu"] = jnp.sum(d_silu, axis=1).reshape(1, w)
        return sums

    back1 = norm_back(
        d_hidden1, norm1, rstd1, [mod[m, 1] for m in both], conditioning_back
    )
    grad_inputs = [d_middle[m] + back1[m] for m in both]
    grad_ada, grad_fc1, grad_fc2 = late["grad_ada"], late["fc1"], late["fc2"]
    _, pullback = jax.vjp(jax.nn.silu, conditioning)
    grad_cond = pullback(late["d_silu"])[0]

    grad_proj = first_z[1][:, : 2 * w].astype(f32)
    grad_qkv = jnp.concatenate([first_z[1][:, 2 * w :], last_z[1]], axis=1).astype(f32)
    grad_qkv = jnp.concatenate(
        [
            grad_qkv[:, ((2 * g + m) * 3 + j) * wide : ((2 * g + m) * 3 + j + 1) * wide]
            for m in both
            for j in range(3)
            for g in range(groups)
        ],
        axis=1,
    )

    def stored(gradient):
        return gradient.reshape(gradient.shape[0], 1, -1)

    return (
        pack(results[0]).astype(bf16),
        pack(results[1]).astype(bf16),
        pack(grad_inputs[0]),
        pack(grad_inputs[1]),
        grad_cond,
        stored(grad_ada),
        stored(grad_qkv),
        stored(grad_proj),
        grad_fc1,
        stored(grad_fc2),
    )


def solution(mesh):
    tokens = P("row", "col", None)
    units = P("row", None, "col")
    cond = P("row", "col")
    return jax.shard_map(
        partial(per_device, mesh.shape["row"], mesh.shape["col"]),
        mesh=mesh,
        in_specs=(tokens, tokens, cond, tokens, tokens, tokens, units, tokens, tokens, tokens),
        out_specs=(tokens, tokens, tokens, tokens, cond, tokens, tokens, tokens, units, tokens),
        check_vma=False,
    )
```

```python
from functools import partial

import jax
import jax.numpy as jnp
from jax import lax
from jax.experimental import pallas as pl
from jax.experimental.pallas import tpu as pltpu
from jax.sharding import PartitionSpec as P

MODEL_WIDTH = 1536
HEAD_DIM = 64
FEEDFORWARD_UNITS = 6144
EPSILON = 1e-06
PAIR = 2 * HEAD_DIM
BLOCK = 256
MASKED = -1e30

bf16 = jnp.bfloat16
f32 = jnp.float32


def dot(spec, a, b):
    return jnp.einsum(spec, a, b, preferred_element_type=f32)


def mm_nn(a, b):
    return lax.dot_general(a, b, (((1,), (0,)), ((), ())), preferred_element_type=f32)


def mm_nt(a, b):
    return lax.dot_general(a, b, (((1,), (1,)), ((), ())), preferred_element_type=f32)


def attend_kernel(real, qi, qt, ki, kt, vi, vt, oi, ot, lse, q_s, k_s, v_s, s_0, s_1):
    ni, n, nk = qi.shape[0], q_s.shape[0], k_s.shape[0]
    scale = jnp.asarray(HEAD_DIM**-0.5, bf16)
    q_s[:ni, :] = qi[...] * scale
    q_s[ni:, :] = qt[...] * scale
    k_s[:ni, :] = ki[...]
    k_s[ni:, :] = kt[: nk - ni, :]
    v_s[:, :ni] = vi[...].T
    v_s[:, ni:] = vt[...].T[:, : nk - ni]
    key = lax.broadcasted_iota(jnp.int32, (nk - ni, BLOCK), 0)
    held = (s_0, s_1)

    def scores(i, h):
        head = slice(h * HEAD_DIM, (h + 1) * HEAD_DIM)
        held[h][...] = mm_nt(k_s[:, head], q_s[i * BLOCK : (i + 1) * BLOCK, head])

    def mix(i, h):
        head = slice(h * HEAD_DIM, (h + 1) * HEAD_DIM)
        s = held[h][...]
        s_i, s_t = s[:ni], jnp.where(key < real, s[ni:], MASKED)
        top = jnp.maximum(
            jnp.max(s_i, axis=0, keepdims=True), jnp.max(s_t, axis=0, keepdims=True)
        )
        e_i, e_t = jnp.exp(s_i - top), jnp.exp(s_t - top)
        total = jnp.sum(e_i, axis=0, keepdims=True) + jnp.sum(e_t, axis=0, keepdims=True)
        part = 1.0 / total
        lse[0, h : h + 1, i * BLOCK : (i + 1) * BLOCK] = top + jnp.log(total)
        return mm_nn(v_s[head, :ni], (e_i * part).astype(bf16)) + mm_nn(
            v_s[head, ni:], (e_t * part).astype(bf16)
        )

    blocks = n // BLOCK
    scores(0, 0)
    for i in range(blocks):
        scores(i, 1)
        first = mix(i, 0)
        if i + 1 < blocks:
            scores(i + 1, 0)
        out = jnp.concatenate([first, mix(i, 1)], axis=0).T.astype(bf16)
        if i * BLOCK < ni:
            oi[i * BLOCK : (i + 1) * BLOCK, :] = out
        else:
            ot[i * BLOCK - ni : (i + 1) * BLOCK - ni, :] = out


def attend_back_kernel(
    real, pairs, qi, qt, ki, kt, vi, vt, di, dt, lse, *rest
):
    out_i, out_t, q_s, k_s, kt_s, v_s, d_s, dq_s, dk_s, dv_s = rest[-10:]
    ni, n, nk = qi.shape[0], q_s.shape[0], k_s.shape[0]
    nt = nk - ni
    scale = HEAD_DIM**-0.5
    q_s[:ni, :] = qi[...] * jnp.asarray(scale, bf16)
    q_s[ni:, :] = qt[...] * jnp.asarray(scale, bf16)
    k_s[:ni, :] = ki[...]
    k_s[ni:, :] = kt[:nt, :]
    kt_s[:, :ni] = ki[...].T
    kt_s[:, ni:] = kt[...].T[:, :nt]
    v_s[:ni, :] = vi[...]
    v_s[ni:, :] = vt[:nt, :]
    d_s[:ni, :] = di[...]
    d_s[ni:, :] = dt[...]
    key = lax.broadcasted_iota(jnp.int32, (nt, BLOCK), 0)
    for i in range(n // BLOCK):
        rows = slice(i * BLOCK, (i + 1) * BLOCK)
        dq = []
        for h in range(2):
            head = slice(h * HEAD_DIM, (h + 1) * HEAD_DIM)
            q, d = q_s[rows, head], d_s[rows, head]
            s = mm_nt(k_s[:, head], q)
            s = jnp.concatenate([s[:ni], jnp.where(key < real, s[ni:], MASKED)], axis=0)
            p = jnp.exp(s - lse[0, h : h + 1, rows])
            t = p * mm_nt(v_s[:, head], d)
            d_scores = (t - p * jnp.sum(t, axis=0, keepdims=True)).astype(bf16)
            dv, dk = mm_nn(p.astype(bf16), d), mm_nn(d_scores, q)
            if i == 0:
                dv_s[:, head] = dv
                dk_s[:, head] = dk
            else:
                dv_s[:, head] += dv
                dk_s[:, head] += dk
            dq.append(mm_nn(kt_s[head, :], d_scores))
        dq_s[:, rows] = jnp.concatenate(dq, axis=0)
    d_q = (dq_s[...] * scale).T.astype(bf16)
    at = pl.program_id(0)

    def lanes(j):
        return pl.ds(pl.multiple_of((j * pairs + at) * PAIR, PAIR), PAIR)

    out_i[:, lanes(0)] = d_q[:ni]
    out_t[:, lanes(0)] = d_q[ni:]
    for j, total in ((1, dk_s), (2, dv_s)):
        out_i[:, lanes(j)] = total[:ni, :].astype(bf16)
        out_t[:nt, lanes(j)] = total[ni:, :].astype(bf16)
        out_t[nt:, lanes(j)] = jnp.zeros((n - nk, PAIR), bf16)


def projection_specs(ni, nt, group, pairs):
    specs = []
    for j in range(3):
        at = lambda p, j=j: (0, (3 * group + j) * pairs + p)
        specs += [pl.BlockSpec((ni, PAIR), at), pl.BlockSpec((nt, PAIR), at)]
    return specs


def attend(image, text, real, group, pairs):
    ni, nt = image.shape[0], text.shape[0]
    n = ni + nt
    nk = ni + (real + 15) // 16 * 16
    at = lambda p: (0, p)
    return pl.pallas_call(
        partial(attend_kernel, real),
        grid=(pairs,),
        in_specs=projection_specs(ni, nt, group, pairs),
        out_specs=[
            pl.BlockSpec((ni, PAIR), at),
            pl.BlockSpec((nt, PAIR), at),
            pl.BlockSpec((1, 2, n), lambda p: (p, 0, 0)),
        ],
        out_shape=[
            jax.ShapeDtypeStruct((ni, pairs * PAIR), bf16),
            jax.ShapeDtypeStruct((nt, pairs * PAIR), bf16),
            jax.ShapeDtypeStruct((pairs, 2, n), f32),
        ],
        scratch_shapes=[
            pltpu.VMEM((n, PAIR), bf16),
            pltpu.VMEM((nk, PAIR), bf16),
            pltpu.VMEM((PAIR, nk), bf16),
            pltpu.VMEM((nk, BLOCK), f32),
            pltpu.VMEM((nk, BLOCK), f32),
        ],
        compiler_params=pltpu.CompilerParams(vmem_limit_bytes=40 * 2**20),
        cost_estimate=pl.CostEstimate(
            flops=pairs * 2 * n * n * 256 * 2 * 2,
            bytes_accessed=pairs * n * PAIR * 2 * 4,
            transcendentals=pairs * 2 * n * n,
        ),
    )(image, text, image, text, image, text)


def attend_back(image, text, real, group, pairs, d_image, d_text, lse, filled):
    ni, nt = image.shape[0], text.shape[0]
    n = ni + nt
    nk = ni + (real + 15) // 16 * 16
    at = lambda p: (0, p)
    one_i, one_t = pl.BlockSpec((ni, PAIR), at), pl.BlockSpec((nt, PAIR), at)
    wide = 3 * pairs * PAIR
    return pl.pallas_call(
        partial(attend_back_kernel, real, pairs),
        grid=(pairs,),
        in_specs=projection_specs(ni, nt, group, pairs)
        + [one_i, one_t, pl.BlockSpec((1, 2, n), lambda p: (p, 0, 0))]
        + [pl.BlockSpec(memory_space=pl.ANY)] * len(filled),
        out_specs=[pl.BlockSpec((n_, wide), lambda p: (0, group)) for n_ in (ni, nt)],
        out_shape=[jax.ShapeDtypeStruct(a.shape, bf16) for a in (image, text)],
        input_output_aliases={9: 0, 10: 1} if filled else {},
        scratch_shapes=[
            pltpu.VMEM((n, PAIR), bf16),
            pltpu.VMEM((nk, PAIR), bf16),
            pltpu.VMEM((PAIR, nk), bf16),
            pltpu.VMEM((nk, PAIR), bf16),
            pltpu.VMEM((n, PAIR), bf16),
            pltpu.VMEM((PAIR, n), f32),
            pltpu.VMEM((nk, PAIR), f32),
            pltpu.VMEM((nk, PAIR), f32),
        ],
        compiler_params=pltpu.CompilerParams(vmem_limit_bytes=40 * 2**20),
        cost_estimate=pl.CostEstimate(
            flops=pairs * 2 * n * n * 256 * 2 * 5,
            bytes_accessed=pairs * n * PAIR * 2 * 8,
            transcendentals=pairs * 2 * n * n,
        ),
    )(image, text, image, text, image, text, d_image, d_text, lse, *filled)


def split_heads(a):
    return a.reshape(a.shape[0], -1, HEAD_DIM)


def plain_attend(image, text, real):
    joined = jnp.concatenate([image, text[:real]], axis=0)
    q, k, v = (split_heads(a) for a in jnp.split(joined, 3, axis=1))
    scores = dot("qhd,khd->hqk", q, k) * HEAD_DIM ** (-0.5)
    top = jnp.max(scores, axis=-1, keepdims=True)
    expo = jnp.exp(scores - top)
    total = jnp.sum(expo, axis=-1, keepdims=True)
    out = dot("hqk,khd->qhd", (expo / total).astype(bf16), v).astype(bf16)
    out = out.reshape(joined.shape[0], -1)
    pad = ((0, text.shape[0] - real), (0, 0))
    ni = image.shape[0]
    return out[:ni], jnp.pad(out[ni:], pad), top + jnp.log(total)


def plain_attend_back(image, text, real, d_image, d_text, lse):
    ni, width = image.shape[0], d_image.shape[1]
    joined = jnp.concatenate([image, text[:real]], axis=0)
    q, k, v = (split_heads(a) for a in jnp.split(joined, 3, axis=1))
    d = split_heads(jnp.concatenate([d_image, d_text[:real]], axis=0))
    factor = HEAD_DIM ** (-0.5)
    probs = jnp.exp(dot("qhd,khd->hqk", q, k) * factor - lse)
    d_v = dot("hqk,qhd->khd", probs.astype(bf16), d)
    d_probs = dot("qhd,khd->hqk", d, v)
    d_scores = probs * (d_probs - jnp.sum(d_probs * probs, axis=-1, keepdims=True))
    d_scores = d_scores.astype(bf16)
    d_q = dot("hqk,khd->qhd", d_scores, k) * factor
    d_k = dot("hqk,qhd->khd", d_scores, q) * factor
    out = jnp.concatenate([g.reshape(-1, width).astype(bf16) for g in (d_q, d_k, d_v)], axis=1)
    return out[:ni], jnp.pad(out[ni:], ((0, text.shape[0] - real), (0, 0)))


def gelu_both(v):
    root = (2.0 / jnp.pi) ** 0.5
    t = jnp.tanh(root * (v + 0.044715 * (v * v * v)))
    half = 0.5 * (1.0 + t)
    slope = half + 0.5 * v * (1.0 - t * t) * (root * (1.0 + 3.0 * 0.044715 * (v * v)))
    return v * half, slope


def row_factors(rows):
    if rows % 4 == 0:
        z = 4 if rows >= 16 else 2
        return z, rows // 2 // z
    return 1, rows // 2


def after(value, *earlier):
    return lax.optimization_barrier((value, *earlier))[0]


def per_device(
    R,
    C,
    image_tokens,
    text_tokens,
    conditioning,
    ada_weight,
    qkv_weight,
    proj_weight,
    fc1_weight,
    fc2_weight,
    image_cotangent,
    text_cotangent,
):
    w = image_tokens.shape[2] // 2
    me_r = lax.axis_index("row")
    me_c = lax.axis_index("col")
    Z, Y = row_factors(R)
    ZY = Z * Y
    my_core = me_r % 2
    my_y = (me_r // 2) % Y
    pair = C == 2
    parity = pair and (R // C) % C == 0
    kernels = w % PAIR == 0
    both = range(2)
    CORE = [(r, r ^ 1) for r in range(R)]
    YSWAP = [(r, r ^ 2) for r in range(R)]
    YGROUPS = [[(z * Y + y) * 2 + c for y in range(Y)] for z in range(Z) for c in range(2)]
    ZGROUPS = [[(z * Y + y) * 2 + c for z in range(Z)] for y in range(Y) for c in range(2)]
    ZYGROUPS = [[2 * k + c for k in range(ZY)] for c in range(2)]
    XSWAP = [(0, 1), (1, 0)]

    def swap(a):
        return lax.ppermute(a, "col", XSWAP)

    def natural(own, other, axis=-1):
        first = jnp.where(me_c == 0, own, other)
        second = jnp.where(me_c == 0, other, own)
        return jnp.concatenate([first, second], axis=axis)

    def send(own):
        if pair:
            return swap(own)
        return lax.all_gather(own, "col", axis=own.ndim - 1, tiled=True)

    def whole(own, got):
        return natural(own, got) if pair else got

    def gather_features(own):
        return whole(own, send(own))

    def col_start(makes, wait=False):
        if pair:
            sent = jnp.concatenate([make(1 - me_c).astype(bf16) for make in makes], axis=0)
            return sent, None if wait else swap(sent)
        sent = jnp.concatenate(
            [jnp.concatenate([make(c) for c in range(C)], axis=-1) for make in makes], axis=0
        )
        return sent, lax.psum_scatter(sent, "col", scatter_dimension=1, tiled=True)

    def col_end(makes, state, *earlier):
        got = after(state[1], *earlier)
        parts = (got[: counts[0]].astype(f32), got[counts[0] :].astype(f32))
        return [make(me_c) + part if pair else part for make, part in zip(makes, parts)]

    def sum_col(a):
        return lax.psum(a, "col")

    def core_start(part):
        sent = part[0]().astype(bf16)
        return sent, lax.ppermute(sent, "row", CORE)

    def y_start(parts, gots):
        owns = [
            [share() + take(got).astype(f32) for share, take in part[1]]
            for part, got in zip(parts, gots)
        ]
        if Y == 2:
            owns = [[own.reshape(Z, own.shape[0] // Z, -1) for own in pieces] for pieces in owns]
            sent = jnp.concatenate([pieces[0].astype(bf16) for pieces in owns], axis=2)
            return sent, [pieces[1] for pieces in owns], lax.ppermute(sent, "row", YSWAP)
        own = jnp.concatenate([pieces[0] for pieces in owns], axis=1)
        own = own.reshape(Z, Y, own.shape[0] // ZY, -1).astype(bf16)
        if Y > 1:
            own = lax.psum_scatter(own, "row", scatter_dimension=1, axis_index_groups=YGROUPS)
        else:
            own = own[:, 0]
        return own, [own], None

    def z_start(states, previous, *earlier):
        pieces = []
        for _, kept, got in states:
            if got is not None:
                got, at, own, kept = after(got, *earlier), 0, kept, []
                for a in own:
                    kept.append((a + got[:, :, at : at + a.shape[2]].astype(f32)).astype(bf16))
                    at += a.shape[2]
            pieces += kept
        kept = jnp.concatenate(pieces, axis=2)
        if Z == 1:
            return [kept, kept[0]]
        if previous is not None:
            kept, previous[1] = lax.optimization_barrier((kept, previous[1]))
        summed = lax.psum_scatter(kept, "row", scatter_dimension=0, axis_index_groups=ZGROUPS)
        return [kept, summed]

    def both_start(parts, gots):
        own = [share() + got.astype(f32) for share, got in zip(parts, gots)]
        own = jnp.concatenate([a.astype(bf16) for a in own], axis=1)
        own = own.reshape(ZY, own.shape[0] // ZY, -1)
        return [
            own,
            lax.psum_scatter(own, "row", scatter_dimension=0, axis_index_groups=ZYGROUPS),
        ]

    def rows_of(a, small=False, plain=Y != 2):
        t, width = a.shape
        blk = width // R
        if plain and not small:
            parts = a.reshape(t, ZY, 2, blk)
            other, own = (
                lax.dynamic_index_in_dim(parts, core, 2, keepdims=False).reshape(t, width // 2)
                for core in (1 - my_core, my_core)
            )
            return other, [own]
        if small:
            at = jnp.arange(width)
            core, y = at // (width // 2), at // (width // 4) % 2
            core = jnp.where(core == 0, 1 - my_core, my_core)
            y = jnp.where(y == 0, 1 - my_y, my_y)
            row = (at // blk % ZY if plain else at // blk % Z * Y + y) * 2 + core
            pick = (row * blk + at % blk)[None, :] == jnp.arange(width)[:, None]
            picked = dot("tp,pq->tq", a, pick.astype(bf16)).astype(bf16)
            half, quarter = width // 2, width // 4
            if plain:
                return picked[:, :half], [picked[:, half:]]
            return picked[:, :half], [picked[:, half : half + quarter], picked[:, -quarter:]]
        parts = a.reshape(t, Z, Y, 2, blk)

        def pick_rows(core, y):
            got = lax.dynamic_index_in_dim(parts, core, 3, keepdims=False)
            return lax.dynamic_index_in_dim(got, y, 2, keepdims=False).reshape(t, Z * blk)

        other = jnp.concatenate(
            [pick_rows(1 - my_core, 1 - my_y), pick_rows(1 - my_core, my_y)], axis=1
        )
        return other, [pick_rows(my_core, 1 - my_y), pick_rows(my_core, my_y)]

    def rows_of_both(pair_of, **how):
        return [rows_of(pair_of[0], **how), rows_of(pair_of[1], small=True, **how)]

    def product_part(rows, b):
        other, own = rows
        size = other.shape[1] // len(own)

        def share(a):
            return lambda: dot("tp,tn->pn", a, b)

        def take(i):
            return lambda got: got[i * size : (i + 1) * size]

        return share(other), [(share(a), take(i)) for i, a in enumerate(own)]

    def unpack(packed):
        rows = packed.reshape(packed.shape[0], 2 * w)
        return jnp.concatenate([rows[:, :w], rows[:, w:]], axis=0)

    def pack(plain):
        half = plain.shape[0] // 2
        return jnp.concatenate([plain[:half], plain[half:]], axis=1).reshape(half, 1, 2 * w)

    def gather_rows(a, order=None):
        return lax.all_gather(a, "row", axis=1, tiled=True, axis_index_groups=order)

    total = w // PAIR
    groups = (3 if total % 3 == 0 else 1) if kernels else 1
    pairs = total // groups
    wide = w // groups
    fan = MODEL_WIDTH // R
    qkv_shard = qkv_weight.reshape(fan, 6 * w)
    proj_shard = proj_weight.reshape(fan, 2 * w)
    first_shard = jnp.stack(
        [
            jnp.concatenate(
                [
                    qkv_shard[:, (3 * m + j) * w + g * wide :][:, :wide].astype(bf16)
                    for g in range(groups)
                    for j in range(3)
                ]
                + [
                    proj_shard[:, m * w : (m + 1) * w].astype(bf16),
                ],
                axis=1,
            )
            for m in both
        ]
    )
    first_full = gather_rows(first_shard)
    qkv_full = [first_full[m, :, : 3 * w] for m in both]
    proj_full = [first_full[m, :, 3 * w :] for m in both]

    silu_own = jax.nn.silu(conditioning).astype(bf16).reshape(R // C, 1, fan)
    silu_sent = jnp.broadcast_to(silu_own[None], (C, R // C, C, fan)).reshape(R * C, fan)
    silu_got = lax.all_to_all(silu_sent, ("row", "col"), 0, 0, tiled=True).reshape(R, C, fan)
    silu_rows = lax.dynamic_index_in_dim(silu_got, me_r // (R // C), 1, keepdims=False)
    ada_shard = ada_weight.reshape(fan, 12 * w).astype(bf16)
    mod = lax.all_to_all(dot("sd,de->se", silu_rows, ada_shard), "row", 0, 0, tiled=True)
    mod = jnp.sum(mod, axis=0).reshape(2, 6, w)

    packed = (image_tokens, text_tokens)
    packed_got = None
    if pair:
        packed_got = swap(jnp.concatenate(packed, axis=0))
        packed_got = [packed_got[: packed[0].shape[0]], packed_got[packed[0].shape[0] :]]
    first_mod = gather_features(mod[:, 0:2].reshape(4, w)).reshape(2, 2, MODEL_WIDTH)
    inputs = [unpack(p).astype(f32) for p in packed]
    cotangents = [unpack(p).astype(f32) for p in (image_cotangent, text_cotangent)]
    counts = [a.shape[0] for a in inputs]
    real = counts[1]
    padding = -(counts[0] + real) % BLOCK
    d_branch2 = [(mod[m, 5] * cotangents[m]).astype(bf16) for m in both]

    fc1_weight, fc2_weight = lax.optimization_barrier((fc1_weight, fc2_weight, silu_got))[:2]
    fc1_shard = jnp.stack([fc1_weight[:, m] for m in both]).astype(bf16)
    blk2 = fc2_weight.shape[0]
    fc2_shard = fc2_weight.reshape(blk2, 2 * w)
    fc2_shard = jnp.stack([fc2_shard[:, m * w : (m + 1) * w] for m in both]).astype(bf16)
    units = fc1_shard.shape[2]
    blocks = units // blk2

    if parity:
        half = blocks // 2
        MOVES = [(r * C + c, ((r // C) * C + c) * C + r % C) for r in range(R) for c in range(C)]
        MOVES = [(a, b) for a, b in MOVES if a != b]
        stays = me_r % C == me_c
        ORDER = [[k * C + c for c in range(C) for k in range(R // C)]]

        def move_units(a, *earlier):
            moved = lax.ppermute(a, ("row", "col"), MOVES)
            return jnp.where(stays, a, after(moved, *earlier) if earlier else moved)

        unmove_units = move_units
        group = fc1_shard.reshape(2, fan, half, 2, blk2)
        mine = lax.dynamic_index_in_dim(group, me_c, 3, keepdims=False)
        theirs = swap(lax.dynamic_index_in_dim(group, 1 - me_c, 3, keepdims=False))

        def moved_columns(*earlier):
            return natural(mine, after(theirs, *earlier), axis=2).reshape(fc1_shard.shape)

        def unmove_columns(g):
            g = g.reshape(fan, 2, blocks, blk2)
            first, second = g[:, :, :half], g[:, :, half:]
            mine = jnp.where(me_c == 0, first, second)
            theirs = swap(jnp.where(me_c == 0, second, first))
            even = jnp.where(me_c == 0, mine, theirs)
            odd = jnp.where(me_c == 0, theirs, mine)
            return jnp.stack([even, odd], axis=3).reshape(fan, 2, units)

    else:
        MOVES = [
            (r * C + c, (c * (R // C) + r % (R // C)) * C + r // (R // C))
            for r in range(R)
            for c in range(C)
        ]
        ORDER = None

        def move_units(a, *earlier):
            return lax.ppermute(a, ("row", "col"), MOVES)

        def moved_columns(*earlier):
            return fc1_shard

        def unmove_units(a):
            return lax.ppermute(a, ("row", "col"), [(b, a) for a, b in MOVES])

        def unmove_columns(g):
            return g


    def padded(a):
        return jnp.pad(a, ((0, padding), (0, 0)))

    if pair:
        inputs_full = [natural(unpack(packed[m]), unpack(packed_got[m])) for m in both]
    else:
        inputs_full = [gather_features(unpack(p)) for p in packed]

    mean1, rstd1, hidden1 = [], [], []
    for m in both:
        x = inputs_full[m].astype(f32)
        mean = jnp.sum(x, axis=-1, keepdims=True) / MODEL_WIDTH
        meansq = jnp.sum(x * x, axis=-1, keepdims=True) / MODEL_WIDTH
        rstd = lax.rsqrt(meansq - mean * mean + EPSILON)
        mean1.append(mean)
        rstd1.append(rstd)
        hidden1.append(
            ((x - mean) * rstd * (1.0 + first_mod[m, 1]) + first_mod[m, 0]).astype(bf16)
        )
    hidden1[1] = padded(hidden1[1])
    norm1 = [(inputs[m] - mean1[m]) * rstd1[m] for m in both]
    fc1_moved = moved_columns(*hidden1)
    fc1_full = gather_rows(fc1_moved)
    d_branch2_own = jnp.concatenate(d_branch2, axis=0)
    d_branch2_got = send(d_branch2_own)
    fc2_shard = after(fc2_shard, d_branch2_got)
    hidden1_in = [after(hidden1[0], d_branch2_got), hidden1[1]]
    projected = [dot("td,de->te", hidden1_in[m], qkv_full[m]).astype(bf16) for m in both]
    fc2_moved = move_units(fc2_shard, *projected)
    fc2_full = gather_rows(fc2_moved, ORDER).reshape(2, C, units, w)

    attended, attended_got, lse = [], [], []
    for g in range(groups):
        text = projected[1]
        if g > 1:
            text = after(text, attended_got[g - 2])
        if kernels:
            out_i, out_t, saved = attend(projected[0], text, real, g, pairs)
        else:
            out_i, out_t, saved = plain_attend(projected[0], text, real)
        attended.append(jnp.concatenate([out_i, out_t[:real]], axis=0))
        attended_got.append(send(attended[g]))
        lse.append(saved)
    attended_full = whole(
        jnp.concatenate(attended, axis=1), jnp.concatenate(attended_got, axis=1)
    )
    attended_full = [attended_full[: counts[0]], attended_full[counts[0] :]]
    attended_rows, hidden1_rows = rows_of_both(attended_full), rows_of_both(hidden1)

    branch1 = [dot("te,eb->tb", attended_full[m], proj_full[m]) for m in both]
    middle = [inputs[m] + mod[m, 2] * branch1[m] for m in both]

    def token_sums(firsts, seconds):
        own = jnp.concatenate(
            [
                jnp.stack([jnp.sum(firsts[m], axis=-1), jnp.sum(seconds[m], axis=-1)])
                for m in both
            ],
            axis=1,
        )
        sums = sum_col(own) / MODEL_WIDTH
        parts = (sums[:, : counts[0]], sums[:, counts[0] :])
        return [(p[0][:, None], p[1][:, None]) for p in parts]

    stats = token_sums(middle, [a * a for a in middle])
    rstd2 = [lax.rsqrt(sq - mean * mean + EPSILON) for mean, sq in stats]
    norm2 = [(middle[m] - stats[m][0]) * rstd2[m] for m in both]
    hidden2 = [(norm2[m] * (1.0 + mod[m, 4]) + mod[m, 3]).astype(bf16) for m in both]
    hidden2[0] = after(hidden2[0], hidden2[1])
    hidden2_got = [send(a) for a in hidden2]
    hidden2_got[0], attended_rows, hidden1_rows = lax.optimization_barrier(
        (hidden2_got[0], attended_rows, hidden1_rows)
    )
    hidden2_full = [whole(a, got) for a, got in zip(hidden2, hidden2_got)]
    d_branch2_full = whole(d_branch2_own, after(d_branch2_got, hidden2[0]))
    d_branch2_full = [d_branch2_full[: counts[0]], d_branch2_full[counts[0] :]]
    hidden2_rows = rows_of_both(hidden2_full, plain=True)
    preact = [dot("td,df->tf", hidden2_full[m], fc1_full[m]) for m in both]
    pairs_of = [gelu_both(a) for a in preact]
    activated = [a.astype(bf16) for a, _ in pairs_of]
    slope = [s for _, s in pairs_of]

    def fc2_part(m, act):
        def share(a, core):
            grad = d_branch2_full[m]
            if parity:
                grad = lax.dynamic_slice_in_dim(grad, core * w, w, 1)
                return lambda: dot("tf,te->fe", a, grad)
            shares = [dot("tf,te->fe", a, grad[:, c * w : (c + 1) * w]) for c in range(C)]
            shares = jnp.concatenate(shares, axis=0).reshape(ZY, 2, blk2, w)
            one = lax.dynamic_index_in_dim(shares, core, 1, keepdims=False)
            return lambda: one.reshape(ZY * blk2, w)

        return share(act, 1 - my_core), share(act, my_core)

    fc2_core = [core_start(fc2_part(m, activated[m])) for m in both]
    act_later = [after(activated[m], *[s[0] for s in fc2_core]) for m in both]
    fc2_z = both_start(
        [fc2_part(m, act_later[m])[1] for m in both], [s[1] for s in fc2_core]
    )
    grads = [after(d_branch2_full[m], fc2_z[0]) for m in both]
    none = jnp.minimum(me_r, 0)
    d_activated = [
        dot(
            "tce,cfe->tf",
            grads[m].reshape(-1, C, w),
            lax.dynamic_slice(fc2_full, (m + none, 0, 0, 0), (1, C, units, w))[0],
        )
        for m in both
    ]
    d_preact = [(d_activated[m] * slope[m]).astype(bf16) for m in both]

    def hidden2_make(m, d):
        return lambda c: dot(
            "tf,df->td", d, lax.dynamic_slice(fc1_full, (m, c * w, 0), (1, w, units))[0]
        )

    hidden2_col = col_start([hidden2_make(m, d_preact[m]) for m in both])

    d_next = [after(d_preact[m], hidden2_col[0]) for m in both]
    fc1_core = [core_start(product_part(hidden2_rows[m], d_next[m])) for m in both]
    fc1_sent = [s[0] for s in fc1_core]

    def branch2_make(m, act):
        return lambda c: dot(
            "tf,fe->te", act, lax.dynamic_slice(fc2_full, (m, c, 0, 0), (1, 1, units, w))[0, 0]
        )

    d_next = [after(d_next[m], *fc1_sent) for m in both]
    fc1_z = both_start(
        [product_part(hidden2_rows[m], d_next[m])[1][0][0] for m in both],
        [s[1] for s in fc1_core],
    )
    d_hidden2 = col_end(
        [hidden2_make(m, d_next[m]) for m in both], hidden2_col, fc1_z[0]
    )
    d_hidden2 = [d.astype(bf16).astype(f32) for d in d_hidden2]

    def norm_back(d_hidden, norm, rstd, scale, between=None):
        d_norm = [d_hidden[m] * (1.0 + scale[m]) for m in both]
        sums = token_sums(d_norm, [d_norm[m] * norm[m] for m in both])
        if between is not None:
            sums = between(sums)
        return [rstd[m] * (d_norm[m] - sums[m][0] - norm[m] * sums[m][1]) for m in both]

    back2 = norm_back(d_hidden2, norm2, rstd2, [mod[m, 4] for m in both])
    d_middle = [cotangents[m] + back2[m] for m in both]
    d_branch1 = [(mod[m, 2] * d_middle[m]).astype(bf16) for m in both]

    def attended_make(m, g, d):
        return lambda c: dot(
            "tv,yv->ty",
            d,
            lax.dynamic_slice(first_full, (m, c * w + g * wide, 3 * w), (1, wide, w))[0],
        )

    attended_col = [col_start([attended_make(m, 0, d_branch1[m]) for m in both])]
    act_last = [after(activated[m], attended_col[0][0]) for m in both]
    branch2_col = col_start([branch2_make(m, act_last[m]) for m in both], wait=True)
    d_last = [after(d_branch1[m], attended_col[0][0]) for m in both]
    proj_core = [core_start(product_part(attended_rows[m], d_last[m])) for m in both]

    d_projected, qkv_core, qkv_y = [], [], []
    later = [s[0] for s in proj_core] + [branch2_col[0]]

    def qkv_part(g, m):
        return product_part(hidden1_rows[m], d_projected[m][:, 3 * wide * g :][:, : 3 * wide])

    def hidden1_make(m, d):
        return lambda c: dot(
            "te,de->td", d, lax.dynamic_slice(first_full, (m, c * w, 0), (1, w, 3 * w))[0]
        )

    for g in range(groups):
        makes = [attended_make(m, g, d_branch1[m]) for m in both]
        d_attended = [d.astype(bf16) for d in col_end(makes, attended_col[g], *d_projected)]
        if g + 1 < groups:
            d_following = [after(d_branch1[m], *d_attended) for m in both]
            attended_col.append(
                col_start([attended_make(m, g + 1, d_following[m]) for m in both])
            )
            later = [*later, attended_col[g + 1][0]]
        if pair and g == max(groups - 2, 0):
            branch2_col = branch2_col[0], swap(after(branch2_col[0], attended_col[-1][0]))
        d_attended[1] = after(padded(d_attended[1]), *later)
        if g == 1:
            d_attended[1], fc2_z[1] = lax.optimization_barrier((d_attended[1], fc2_z[1]))
        if kernels:
            filled = d_projected
            if g:
                filled = [after(a, *later) for a in d_projected]
            outs = attend_back(
                projected[0], projected[1], real, g, pairs, *d_attended, lse[g], filled
            )
        else:
            outs = plain_attend_back(projected[0], projected[1], real, *d_attended, lse[g])
        d_projected = list(outs)
        done = list(d_projected)
        later = []
        if g + 1 < groups:
            qkv_core.append([core_start(qkv_part(g, m)) for m in both])
            later += [qkv_core[g][m][0] for m in both]
        if g == 1:
            gots = [after(s[1], *done) for s in proj_core + qkv_core[0]]
            parts = [product_part(attended_rows[m], d_last[m]) for m in both]
            proj_y = y_start(parts + [qkv_part(0, m) for m in both], gots)
            qkv_y.append(None)
            later.append(proj_y[0])
    if groups == 1:
        proj_y = y_start(
            [product_part(attended_rows[m], d_last[m]) for m in both], [s[1] for s in proj_core]
        )

    got = after(branch2_col[1], *done)
    d_projected[1], got = lax.optimization_barrier((d_projected[1], got))
    branch2_col = branch2_col[0], got
    d_all = [d_projected[m][: counts[m]] for m in both]
    hidden1_makes = [hidden1_make(m, d_all[m]) for m in both]
    hidden1_col = col_start(hidden1_makes)
    g = groups - 1
    d_projected = [after(a, hidden1_col[0]) for a in d_projected]
    qkv_core.append([core_start(qkv_part(g, m)) for m in both])
    for g in range(len(qkv_y), groups):
        qkv_y.append(y_start([qkv_part(g, m) for m in both], [s[1] for s in qkv_core[g]]))
    act_last = [after(act_last[m], hidden1_col[0]) for m in both]
    branch2 = col_end([branch2_make(m, act_last[m]) for m in both], branch2_col)
    results = [middle[m] + mod[m, 5] * branch2[m] for m in both]
    d_gate2 = [jnp.sum(cotangents[m] * branch2[m], axis=0) for m in both]

    d_gate1 = [jnp.sum(d_middle[m] * branch1[m], axis=0) for m in both]
    d_shift2 = [jnp.sum(d_hidden2[m], axis=0) for m in both]
    d_scale2 = [jnp.sum(d_hidden2[m] * norm2[m], axis=0) for m in both]

    d_hidden1 = col_end(hidden1_makes, hidden1_col)
    d_hidden1 = [d.astype(bf16) for d in d_hidden1]
    first_z = z_start([proj_y], None, d_hidden1[1])
    d_hidden1[0], fc2_summed = lax.optimization_barrier((d_hidden1[0], fc2_z[1]))
    d_hidden1 = [d.astype(f32) for d in d_hidden1]
    d_shift1 = [jnp.sum(d_hidden1[m], axis=0) for m in both]
    d_scale1 = [jnp.sum(d_hidden1[m] * norm1[m], axis=0) for m in both]
    d_mod = jnp.concatenate(
        [
            part[m].reshape(1, w)
            for m in both
            for part in (d_shift1, d_scale1, d_gate1, d_shift2, d_scale2, d_gate2)
        ],
        axis=1,
    ).astype(bf16)
    d_mod, fc1_summed = lax.optimization_barrier((d_mod, fc1_z[1]))
    last_z = z_start([state for state in qkv_y if state], None, d_mod)
    d_mod_all = lax.all_to_all(jnp.broadcast_to(d_mod, (R, 12 * w)), "row", 0, 0, tiled=True)
    late = {}

    def conditioning_back(sums):
        sums, got = lax.optimization_barrier((sums, d_mod_all))
        late["grad_ada"] = dot("sd,se->de", silu_rows, got)
        d_silu = dot("se,de->sd", got, ada_shard)
        late["fc2"] = unmove_units(fc2_summed.astype(f32))
        late["fc1"] = unmove_columns(fc1_summed.astype(f32)).reshape(fan, 2, units)
        sums, d_silu = lax.optimization_barrier((sums, d_silu))
        d_silu = jnp.broadcast_to(d_silu[:, None], (R, C, fan)).reshape(R * C, fan)
        d_silu = lax.all_to_all(d_silu, ("row", "col"), 0, 0, tiled=True)
        d_silu = d_silu.reshape(C, R // C, C, fan)
        d_silu = lax.dynamic_index_in_dim(d_silu, me_c, 0, keepdims=False)
        late["d_silu"] = jnp.sum(d_silu, axis=1).reshape(1, w)
        return sums

    back1 = norm_back(
        d_hidden1, norm1, rstd1, [mod[m, 1] for m in both], conditioning_back
    )
    grad_inputs = [d_middle[m] + back1[m] for m in both]
    grad_ada, grad_fc1, grad_fc2 = late["grad_ada"], late["fc1"], late["fc2"]
    _, pullback = jax.vjp(jax.nn.silu, conditioning)
    grad_cond = pullback(late["d_silu"])[0]

    grad_proj = first_z[1][:, : 2 * w].astype(f32)
    grad_qkv = jnp.concatenate([first_z[1][:, 2 * w :], last_z[1]], axis=1).astype(f32)
    grad_qkv = jnp.concatenate(
        [
            grad_qkv[:, ((2 * g + m) * 3 + j) * wide : ((2 * g + m) * 3 + j + 1) * wide]
            for m in both
            for j in range(3)
            for g in range(groups)
        ],
        axis=1,
    )

    def stored(gradient):
        return gradient.reshape(gradient.shape[0], 1, -1)

    return (
        pack(results[0]).astype(bf16),
        pack(results[1]).astype(bf16),
        pack(grad_inputs[0]),
        pack(grad_inputs[1]),
        grad_cond,
        stored(grad_ada),
        stored(grad_qkv),
        stored(grad_proj),
        grad_fc1,
        stored(grad_fc2),
    )


def solution(mesh):
    tokens = P("row", "col", None)
    units = P("row", None, "col")
    cond = P("row", "col")
    return jax.shard_map(
        partial(per_device, mesh.shape["row"], mesh.shape["col"]),
        mesh=mesh,
        in_specs=(tokens, tokens, cond, tokens, tokens, tokens, units, tokens, tokens, tokens),
        out_specs=(tokens, tokens, tokens, tokens, cond, tokens, tokens, tokens, units, tokens),
        check_vma=False,
    )
```
